32 devices in a mesh: groups: 2 (over y), seq: 4 (over x, core), tensor: 4 (over z).
Axes of the slice: x: 2, y: 2, z: 4, core: 2. Of those that a mesh axis runs over, the one named last changes fastest.
Arguments:
- spectrum: bfloat16 [12288, 80], P(('groups', 'seq')), parts along dimension 0, may hold values from -6 to 6
- conv_weight: bfloat16 [3, 80, 1536], P(None, None, 'tensor'), may hold values from -0.375 to 0.375
- conv_bias: float32 [1536], P('tensor'), may hold values from -3 to 3
- depth_weight: float32 [3, 1536], replicated, may hold values from -3 to 3
- depth_bias: float32 [1536], replicated, may hold values from -3 to 3
- mix_gain: float32 [1536], replicated, may hold values from 0.5 to 1.5
- mix_shift: float32 [1536], replicated, may hold values from -3 to 3
- feed_gain: float32 [1536], replicated, may hold values from 0.5 to 1.5
- feed_shift: float32 [1536], replicated, may hold values from -3 to 3
- heads_weight: bfloat16 [1536, 4608], P(None, 'tensor'), may hold values from -0.15625 to 0.15625
- heads_bias: float32 [4608], P('tensor'), may hold values from -3 to 3
- up_weight: bfloat16 [1536, 6144], P(None, 'tensor'), may hold values from -0.15625 to 0.15625
- up_bias: float32 [6144], P('tensor'), may hold values from -3 to 3
Outputs:
- attention_inputs: bfloat16 [3072, 4608], P(('groups', 'seq'), 'tensor'), parts along dimension 0
- feed_hidden: bfloat16 [3072, 6144], P(('groups', 'seq'), 'tensor'), parts along dimension 0
The draws below stay inside these ranges and needn't reach their ends.
There are 2 independent parts, one for each index of `groups`. The reference program is written for one: setup_inputs(seed, part) draws one part's arguments, and reference() takes and returns one part's arrays. A program takes and returns all parts, laid end to end along the dimension named above; an argument that names none is the same for every part. Nothing has to cross between parts.
All inputs are finite; a program needn't handle non-finite values.
Results may differ from the reference program's by a relative error of at most 0.009.
Values may be sent and summed in bfloat16 or wider, within the bound.
A program may use at most 128 MiB of HBM per device.

```python
import jax
import jax.numpy as jnp
from jax import lax

D = 1536
FF = 6144
MELS = 80
MEL_FRAMES = 6144


def shard_levels(rng, extent, pieces, low, high):
    def one(dim, parts):
        draws = jax.random.uniform(jax.random.fold_in(jax.random.fold_in(rng, 6), dim), (parts,), jnp.float32, low / len(pieces), high / len(pieces))
        return jnp.repeat(jnp.exp(draws), extent[dim] // parts).reshape((-1,) + (1,) * (len(extent) - dim - 1))

    gain = one(*pieces[0])
    for cut in pieces[1:]:
        gain = gain * one(*cut)
    return gain


def noise(rng, shape, spread, reach, cuts=(), kind=jnp.bfloat16):
    values = jax.random.normal(rng, shape, jnp.float32) * spread
    if len(cuts) > 0:
        values = shard_levels(rng, shape, cuts, -0.22, 0.18) * values
    return jnp.clip(values, min=-reach, max=reach).astype(kind)


def setup_inputs(seed: int = 0, part: int = 0) -> dict:
    splits = jax.random.split(jax.random.key(seed), 14)
    part_splits = jax.random.split(jax.random.fold_in(splits[13], part), 14)
    spectrum = noise(part_splits[0], (MEL_FRAMES, MELS), 1.0, 6.0, ((0, 4),))
    conv_weight = noise(splits[1], (3, MELS, D), (3 * MELS) ** -0.5, 0.375, ((2, 4),))
    conv_bias = noise(splits[2], (D,), 0.5, 3.0, ((0, 4),), jnp.float32)
    depth_weight = noise(splits[3], (3, D), 0.6, 3.0, (), jnp.float32)
    depth_bias = noise(splits[4], (D,), 0.5, 3.0, (), jnp.float32)
    mix_gain = jnp.clip(jax.random.uniform(splits[5], (D,), jnp.float32, 0.5, 1.5), 0.5, 1.5)
    mix_shift = noise(splits[6], (D,), 0.5, 3.0, (), jnp.float32)
    feed_gain = jnp.clip(jax.random.uniform(splits[7], (D,), jnp.float32, 0.5, 1.5), 0.5, 1.5)
    feed_shift = noise(splits[8], (D,), 0.5, 3.0, (), jnp.float32)
    heads_weight = noise(splits[9], (D, 3 * D), D ** -0.5, 0.15625, ((1, 4),))
    heads_bias = noise(splits[10], (3 * D,), 0.5, 3.0, ((0, 4),), jnp.float32)
    up_weight = noise(splits[11], (D, FF), D ** -0.5, 0.15625, ((1, 4),))
    up_bias = noise(splits[12], (FF,), 0.5, 3.0, ((0, 4),), jnp.float32)
    return dict(spectrum=spectrum, conv_weight=conv_weight, conv_bias=conv_bias, depth_weight=depth_weight, depth_bias=depth_bias, mix_gain=mix_gain, mix_shift=mix_shift, feed_gain=feed_gain, feed_shift=feed_shift, heads_weight=heads_weight, heads_bias=heads_bias, up_weight=up_weight, up_bias=up_bias)


epsilon = 1e-05

def layer_norm(summed):
    row_mean = lax.optimization_barrier(jnp.mean(summed, axis=-1, keepdims=True))
    centred = summed - row_mean
    variance = lax.optimization_barrier(jnp.mean(centred * centred, axis=-1, keepdims=True))
    return centred * lax.rsqrt(variance + epsilon)

def reference(spectrum, conv_weight, conv_bias, depth_weight, depth_bias, mix_gain, mix_shift, feed_gain, feed_shift, heads_weight, heads_bias, up_weight, up_bias):
    even_rows = spectrum[0::2]
    odd_rows = spectrum[1::2]
    prior_rows = jnp.concatenate([jnp.zeros_like(odd_rows[:1]), odd_rows[:-1]], axis=0)
    stacked = jnp.concatenate([prior_rows, even_rows, odd_rows], axis=1)
    flat_weight = conv_weight.reshape(3 * MELS, D)
    channels = jax.nn.relu(jnp.dot(stacked, flat_weight, preferred_element_type=jnp.float32) + conv_bias).astype(jnp.bfloat16)
    even_half = channels[0::2].astype(jnp.float32)
    odd_half = channels[1::2].astype(jnp.float32)
    prior_half = jnp.concatenate([jnp.zeros_like(odd_half[:1]), odd_half[:-1]], axis=0)
    summed = prior_half * depth_weight[0] + even_half * depth_weight[1] + odd_half * depth_weight[2] + depth_bias
    subsampled = jax.nn.relu(summed).astype(jnp.bfloat16)
    normed = layer_norm(subsampled.astype(jnp.float32))
    mix_input = (normed * mix_gain + mix_shift).astype(jnp.bfloat16)
    feed_input = (normed * feed_gain + feed_shift).astype(jnp.bfloat16)
    attention_inputs = (jnp.dot(mix_input, heads_weight, preferred_element_type=jnp.float32) + heads_bias).astype(jnp.bfloat16)
    raised = jnp.dot(feed_input, up_weight, preferred_element_type=jnp.float32) + up_bias
    feed_hidden = jax.nn.silu(raised).astype(jnp.bfloat16)
    return (attention_inputs, feed_hidden)
```

```python
import functools

import jax
import jax.numpy as jnp
from jax import lax
from jax.experimental import pallas as pl
from jax.experimental.pallas import tpu as pltpu
from jax.sharding import PartitionSpec as P

epsilon = 1e-05
HALO = 16
MESH = pl.DeviceIdType.MESH


def passed_along(value, axis, steps):
    count = lax.axis_size(axis)
    initial, last = (max(0, -steps), min(count, count - steps))
    return lax.ppermute(value, axis, [(source, source + steps) for source in range(initial, last)])


def conv_rows(prior_rows, even_rows, odd_rows, conv_weight, conv_bias):
    stacked = jnp.concatenate([prior_rows, even_rows, odd_rows], axis=1)
    flat_weight = conv_weight.reshape(-1, conv_weight.shape[2])
    summed = jnp.dot(stacked, flat_weight, preferred_element_type=jnp.float32) + conv_bias
    return jax.nn.relu(summed).astype(jnp.bfloat16)


def first_conv(spectrum, prior_row, conv_weight, conv_bias):
    even_rows = spectrum[0::2]
    odd_rows = spectrum[1::2]
    prior_rows = jnp.concatenate([prior_row, odd_rows[:-1]], axis=0)
    return conv_rows(prior_rows, even_rows, odd_rows, conv_weight, conv_bias)


def depth_conv(channels, prior_row, depth_weight, depth_bias):
    even_half = channels[0::2].astype(jnp.float32)
    odd_half = channels[1::2].astype(jnp.float32)
    prior_half = jnp.concatenate([prior_row.astype(jnp.float32), odd_half[:-1]], axis=0)
    summed = (
        prior_half * depth_weight[0]
        + even_half * depth_weight[1]
        + odd_half * depth_weight[2]
        + depth_bias
    )
    return jax.nn.relu(summed).astype(jnp.bfloat16)


def plain_device(
    spectrum,
    conv_weight,
    conv_bias,
    depth_weight,
    depth_bias,
    mix_gain,
    mix_shift,
    feed_gain,
    feed_shift,
    heads_weight,
    heads_bias,
    up_weight,
    up_bias,
):
    mel_prior = passed_along(spectrum[-1:], "seq", 1)
    channels = first_conv(spectrum, mel_prior, conv_weight, conv_bias)
    own_width = channels.shape[1]
    lane_index = lax.axis_index("tensor")
    own_weight = lax.dynamic_slice_in_dim(depth_weight, lane_index * own_width, own_width, 1)
    own_bias = lax.dynamic_slice_in_dim(depth_bias, lane_index * own_width, own_width, 0)
    prior_row = passed_along(channels[-1:], "seq", 1)
    reduced = depth_conv(channels, prior_row, own_weight, own_bias)
    subsampled = lax.all_to_all(reduced, "tensor", split_axis=0, concat_axis=1, tiled=True)
    frames_float = lax.all_gather(subsampled, "tensor", axis=0, tiled=True).astype(jnp.float32)
    row_mean = jnp.mean(frames_float, axis=-1, keepdims=True)
    centred = frames_float - row_mean
    variance = jnp.mean(centred * centred, axis=-1, keepdims=True)
    normed = centred * lax.rsqrt(variance + epsilon)
    mix_input = (normed * mix_gain + mix_shift).astype(jnp.bfloat16)
    feed_input = (normed * feed_gain + feed_shift).astype(jnp.bfloat16)
    heads_out = (
        jnp.dot(mix_input, heads_weight, preferred_element_type=jnp.float32) + heads_bias
    ).astype(jnp.bfloat16)
    raised = jnp.dot(feed_input, up_weight, preferred_element_type=jnp.float32) + up_bias
    gated = jax.nn.silu(raised).astype(jnp.bfloat16)
    return heads_out, gated


def tiles_of(width, tile):
    whole = width // tile
    return whole, width - whole * tile


def front_kernel(
    count,
    mels,
    spectrum,
    conv_weight,
    conv_bias,
    depth_weight,
    depth_bias,
    mix_gain,
    mix_shift,
    feed_gain,
    feed_shift,
    heads_bias,
    up_bias,
    heads_hbm,
    up_hbm,
    heads_out,
    up_out,
    heads_w,
    up_w,
    gathered,
    halo,
    frames,
    stacked,
    subsampled,
    mix_input,
    feed_input,
    heads_stage,
    up_stage,
    load_sem,
    halo_sem,
    send1,
    recv1,
    send2,
    recv2,
    send3,
    recv3,
    heads_sem,
    up_sem,
):
    group = lax.axis_index("groups")
    span = lax.axis_index("seq")
    lane = lax.axis_index("tensor")
    taps, width = conv_weight.shape
    depth = gathered.shape[1]
    piece_rows = depth // 8
    rows = subsampled.shape[0]
    mel_rows = spectrum.shape[0]
    channels = subsampled.shape[1]

    core = lax.rem(span, 2)
    sibling = span + 1 - 2 * core
    across = lax.rem(span + 2, 4)
    other = 1 - group
    following = lax.rem(span + 1, 4)

    load_heads = pltpu.make_async_copy(heads_hbm, heads_w, load_sem.at[0])
    load_up = pltpu.make_async_copy(up_hbm, up_w, load_sem.at[1])

    barrier = pltpu.get_barrier_semaphore()
    peers = [(group, span, lax.rem(lane + k, count)) for k in range(1, count)]
    peers += [(group, sibling, lane), (group, across, lane), (group, 3 - span, lane)]
    peers += [(other, span, lane), (other, across, lane)]
    for peer in peers:
        pl.semaphore_signal(barrier, inc=1, device_id=peer, device_id_type=MESH)

    gathered[lane, 0:taps, :] = conv_weight[...]
    bias = conv_bias[...]
    high = bias.astype(jnp.bfloat16).astype(jnp.float32)
    row_id = lax.broadcasted_iota(jnp.int32, (depth - taps, width), 0)
    bias_rows = jnp.where(row_id == 0, high, jnp.where(row_id == 1, bias - high, 0.0))
    gathered[lane, taps:depth, :] = bias_rows.astype(jnp.bfloat16)

    pl.semaphore_wait(barrier, len(peers))

    def piece(shard, owner_group, owner_span):
        start = pl.multiple_of((owner_group * 4 + owner_span) * piece_rows, piece_rows)
        return gathered.at[shard, pl.ds(start, piece_rows), :]

    def send(part, target, send_sem, recv_sem):
        return pltpu.make_async_remote_copy(
            src_ref=part,
            dst_ref=part,
            send_sem=send_sem,
            recv_sem=recv_sem,
            device_id=target,
            device_id_type=MESH,
        )

    sources = [lax.rem(lane + count - k, count) for k in range(1, count)]
    first = []
    for k in range(1, count):
        copy = send(
            piece(lane, group, span),
            (group, span, lax.rem(lane + k, count)),
            send1.at[k - 1],
            recv1.at[k - 1],
        )
        copy.start()
        first.append(copy)
    halo_copy = pltpu.make_async_remote_copy(
        src_ref=spectrum.at[pl.ds(mel_rows - HALO, HALO), :],
        dst_ref=halo,
        send_sem=halo_sem.at[0],
        recv_sem=halo_sem.at[1],
        device_id=(group, following, lane),
        device_id_type=MESH,
    )
    halo_copy.start()
    load_heads.start()
    load_up.start()

    frames[HALO : HALO + mel_rows, 0:mels] = spectrum[...].astype(jnp.float32)

    chips = [(group, across), (other, span), (other, across)]
    second = []
    for k in range(count - 1):
        first[k].wait_recv()
        part = piece(sources[k], group, span)
        copies = []
        for j, (to_group, to_span) in enumerate(chips):
            copies.append(send(part, (to_group, to_span, lane), send2.at[k, j], recv2.at[k, j]))
        copies.append(send(part, (group, sibling, lane), send2.at[k, 3], recv2.at[k, 3]))
        for copy in copies:
            copy.start()
        second.append(copies)

    halo_copy.wait_recv()
    frames[0:HALO, 0:mels] = jnp.where(span == 0, 0.0, halo[...].astype(jnp.float32))

    def tap(offset):
        return frames[pl.ds(HALO + offset, rows, stride=4), :][:, 0:mels]

    taken = {offset: tap(offset) for offset in range(-3, 4)}
    tail_id = lax.broadcasted_iota(jnp.int32, (rows, depth - taps), 1)
    tail = jnp.where(tail_id < 2, 1.0, 0.0)
    row_zero = lax.broadcasted_iota(jnp.int32, (rows, depth - taps), 0) == 0
    start_tail = jnp.where(row_zero & (span == 0), 0.0, tail)
    for which, (base, end) in enumerate(((-3, start_tail), (-1, tail), (1, tail))):
        block = jnp.concatenate([taken[base], taken[base + 1], taken[base + 2], end], axis=1)
        stacked[which * rows : (which + 1) * rows, :] = block.astype(jnp.bfloat16)

    def conv_shard(shard):
        columns = pl.ds(pl.multiple_of(shard * width, 128), width)
        summed = jnp.dot(stacked[...], gathered[shard], preferred_element_type=jnp.float32)
        summed = jnp.maximum(summed, 0.0)
        total = (
            summed[0:rows] * depth_weight[0:1, columns]
            + summed[rows : 2 * rows] * depth_weight[1:2, columns]
            + summed[2 * rows :] * depth_weight[2:3, columns]
            + depth_bias[0:1, columns]
        )
        subsampled[:, columns] = jnp.maximum(total, 0.0).astype(jnp.bfloat16)

    conv_shard(lane)

    third = []
    for k in range(count - 1):
        copies = []
        for j, (to_group, to_span) in enumerate(chips):
            second[k][j].wait_recv()
            copy = send(
                piece(sources[k], to_group, to_span),
                (group, sibling, lane),
                send3.at[k, j],
                recv3.at[k, j],
            )
            copy.start()
            copies.append(copy)
        third.append(copies)

    for k in range(count - 1):
        second[k][3].wait_recv()
        for copy in third[k]:
            copy.wait_recv()
        conv_shard(sources[k])

    chunk = 32

    @pl.loop(0, rows // chunk)
    def _(step):
        some = pl.ds(pl.multiple_of(step * chunk, chunk), chunk)
        values = subsampled[some, :].astype(jnp.float32)
        centred = values - jnp.sum(values, axis=1, keepdims=True) * (1.0 / channels)
        variance = jnp.sum(centred * centred, axis=1, keepdims=True) * (1.0 / channels)
        normed = centred * lax.rsqrt(variance + epsilon)
        mix_input[some, :] = (normed * mix_gain[...] + mix_shift[...]).astype(jnp.bfloat16)
        feed_input[some, :] = (normed * feed_gain[...] + feed_shift[...]).astype(jnp.bfloat16)

    def project(source, weight, bias_row, stage, out, sem, load, activation):
        load.wait()
        tile = 256
        whole, rest = tiles_of(stage.shape[1], tile)

        def columns_copy(index, start, size):
            columns = pl.ds(start, size)
            return pltpu.make_async_copy(stage.at[:, columns], out.at[:, columns], sem.at[index])

        def one(index, start, size):
            columns = pl.ds(start, size)
            summed = jnp.dot(source[...], weight[:, columns], preferred_element_type=jnp.float32)
            summed = summed + bias_row[0:1, columns]
            stage[:, columns] = activation(summed).astype(jnp.bfloat16)
            columns_copy(index, start, size).start()

        @pl.loop(0, whole)
        def _(index):
            one(index, pl.multiple_of(index * tile, tile), tile)

        if rest:
            one(whole, whole * tile, rest)

        def finish():
            for index in range(whole):
                columns_copy(index, index * tile, tile).wait()
            if rest:
                columns_copy(whole, whole * tile, rest).wait()

        return finish

    finish_heads = project(
        mix_input, heads_w, heads_bias, heads_stage, heads_out, heads_sem, load_heads, lambda v: v
    )
    finish_up = project(
        feed_input, up_w, up_bias, up_stage, up_out, up_sem, load_up, jax.nn.silu
    )
    halo_copy.wait_send()
    for copy in first:
        copy.wait_send()
    for copies in second + third:
        for copy in copies:
            copy.wait_send()
    finish_heads()
    finish_up()


def kernel_device(
    count,
    spectrum,
    conv_weight,
    conv_bias,
    depth_weight,
    depth_bias,
    mix_gain,
    mix_shift,
    feed_gain,
    feed_shift,
    heads_weight,
    heads_bias,
    up_weight,
    up_bias,
):
    mel_rows, mels = spectrum.shape
    width = conv_weight.shape[2]
    channels = depth_weight.shape[1]
    taps = 3 * mels
    depth = -(-(taps + 2) // 256) * 256
    rows = mel_rows // 4
    heads_cols, up_cols = heads_weight.shape[1], up_weight.shape[1]
    vmem = pl.BlockSpec(memory_space=pltpu.VMEM)
    anywhere = pl.BlockSpec(memory_space=pl.ANY)
    dma = pltpu.SemaphoreType.DMA
    bf16 = jnp.bfloat16
    return pl.pallas_call(
        functools.partial(front_kernel, count, mels),
        out_shape=(
            jax.ShapeDtypeStruct((rows, heads_cols), bf16),
            jax.ShapeDtypeStruct((rows, up_cols), bf16),
        ),
        in_specs=[vmem] * 11 + [anywhere] * 2,
        out_specs=(anywhere, anywhere),
        scratch_shapes=[
            pltpu.VMEM((channels, heads_cols), bf16),
            pltpu.VMEM((channels, up_cols), bf16),
            pltpu.VMEM((count, depth, width), bf16),
            pltpu.VMEM((HALO, mels), bf16),
            pltpu.VMEM((HALO + mel_rows, 128), jnp.float32),
            pltpu.VMEM((3 * rows, depth), bf16),
            pltpu.VMEM((rows, channels), bf16),
            pltpu.VMEM((rows, channels), bf16),
            pltpu.VMEM((rows, channels), bf16),
            pltpu.VMEM((rows, heads_cols), bf16),
            pltpu.VMEM((rows, up_cols), bf16),
            dma((2,)),
            dma((2,)),
            dma((count - 1,)),
            dma((count - 1,)),
            dma((count - 1, 4)),
            dma((count - 1, 4)),
            dma((count - 1, 3)),
            dma((count - 1, 3)),
            dma((-(-heads_cols // 256),)),
            dma((-(-up_cols // 256),)),
        ],
        compiler_params=pltpu.CompilerParams(
            collective_id=0, has_side_effects=True, vmem_limit_bytes=48 * 2**20
        ),
        cost_estimate=pl.CostEstimate(
            flops=2 * rows * channels * (heads_cols + up_cols + 3 * taps),
            bytes_accessed=2 * (channels + rows) * (heads_cols + up_cols),
            transcendentals=rows * up_cols,
        ),
        name="front",
    )(
        spectrum,
        conv_weight.reshape(taps, width),
        conv_bias.reshape(1, -1),
        depth_weight,
        depth_bias.reshape(1, -1),
        mix_gain.reshape(1, -1),
        mix_shift.reshape(1, -1),
        feed_gain.reshape(1, -1),
        feed_shift.reshape(1, -1),
        heads_bias.reshape(1, -1),
        up_bias.reshape(1, -1),
        heads_weight,
        up_weight,
    )


def solution(mesh):
    in_specs = (
        P(("groups", "seq"), None),
        P(None, None, "tensor"),
        P("tensor"),
        P(),
        P(),
        P(),
        P(),
        P(),
        P(),
        P(None, "tensor"),
        P("tensor"),
        P(None, "tensor"),
        P("tensor"),
    )
    out_specs = (P(("groups", "seq"), "tensor"), P(("groups", "seq"), "tensor"))
    groups, spans, count = (mesh.shape[name] for name in ("groups", "seq", "tensor"))

    def per_device(*arrays):
        width = arrays[1].shape[2]
        if groups == 2 and spans == 4 and count > 1 and width % 128 == 0:
            return kernel_device(count, *arrays)
        return plain_device(*arrays)

    return jax.shard_map(
        per_device, mesh=mesh, in_specs=in_specs, out_specs=out_specs, check_vma=False
    )
```

```python
import functools

import jax
import jax.numpy as jnp
from jax import lax
from jax.experimental import pallas as pl
from jax.experimental.pallas import tpu as pltpu
from jax.sharding import PartitionSpec as P

epsilon = 1e-05
HALO = 128
MESH = pl.DeviceIdType.MESH


def passed_along(value, axis, steps):
    count = lax.axis_size(axis)
    initial, last = (max(0, -steps), min(count, count - steps))
    return lax.ppermute(value, axis, [(source, source + steps) for source in range(initial, last)])


def conv_rows(prior_rows, even_rows, odd_rows, conv_weight, conv_bias):
    stacked = jnp.concatenate([prior_rows, even_rows, odd_rows], axis=1)
    flat_weight = conv_weight.reshape(-1, conv_weight.shape[2])
    summed = jnp.dot(stacked, flat_weight, preferred_element_type=jnp.float32) + conv_bias
    return jax.nn.relu(summed).astype(jnp.bfloat16)


def first_conv(spectrum, prior_row, conv_weight, conv_bias):
    even_rows = spectrum[0::2]
    odd_rows = spectrum[1::2]
    prior_rows = jnp.concatenate([prior_row, odd_rows[:-1]], axis=0)
    return conv_rows(prior_rows, even_rows, odd_rows, conv_weight, conv_bias)


def depth_conv(channels, prior_row, depth_weight, depth_bias):
    even_half = channels[0::2].astype(jnp.float32)
    odd_half = channels[1::2].astype(jnp.float32)
    prior_half = jnp.concatenate([prior_row.astype(jnp.float32), odd_half[:-1]], axis=0)
    summed = (
        prior_half * depth_weight[0]
        + even_half * depth_weight[1]
        + odd_half * depth_weight[2]
        + depth_bias
    )
    return jax.nn.relu(summed).astype(jnp.bfloat16)


def plain_device(
    spectrum,
    conv_weight,
    conv_bias,
    depth_weight,
    depth_bias,
    mix_gain,
    mix_shift,
    feed_gain,
    feed_shift,
    heads_weight,
    heads_bias,
    up_weight,
    up_bias,
):
    mel_prior = passed_along(spectrum[-1:], "seq", 1)
    channels = first_conv(spectrum, mel_prior, conv_weight, conv_bias)
    own_width = channels.shape[1]
    lane_index = lax.axis_index("tensor")
    own_weight = lax.dynamic_slice_in_dim(depth_weight, lane_index * own_width, own_width, 1)
    own_bias = lax.dynamic_slice_in_dim(depth_bias, lane_index * own_width, own_width, 0)
    prior_row = passed_along(channels[-1:], "seq", 1)
    reduced = depth_conv(channels, prior_row, own_weight, own_bias)
    subsampled = lax.all_to_all(reduced, "tensor", split_axis=0, concat_axis=1, tiled=True)
    frames_float = lax.all_gather(subsampled, "tensor", axis=0, tiled=True).astype(jnp.float32)
    row_mean = jnp.mean(frames_float, axis=-1, keepdims=True)
    centred = frames_float - row_mean
    variance = jnp.mean(centred * centred, axis=-1, keepdims=True)
    normed = centred * lax.rsqrt(variance + epsilon)
    mix_input = (normed * mix_gain + mix_shift).astype(jnp.bfloat16)
    feed_input = (normed * feed_gain + feed_shift).astype(jnp.bfloat16)
    heads_out = (
        jnp.dot(mix_input, heads_weight, preferred_element_type=jnp.float32) + heads_bias
    ).astype(jnp.bfloat16)
    raised = jnp.dot(feed_input, up_weight, preferred_element_type=jnp.float32) + up_bias
    gated = jax.nn.silu(raised).astype(jnp.bfloat16)
    return heads_out, gated


def tiles_of(width, tile):
    whole = width // tile
    return whole, width - whole * tile


def front_kernel(
    count,
    spectrum_hbm,
    conv_hbm,
    conv_bias_hbm,
    depth_weight_hbm,
    depth_bias_hbm,
    mix_gain_hbm,
    mix_shift_hbm,
    feed_gain_hbm,
    feed_shift_hbm,
    heads_bias_hbm,
    up_bias_hbm,
    heads_hbm,
    up_hbm,
    heads_out,
    up_out,
    spectrum,
    conv_bias,
    depth_weight,
    depth_bias,
    mix_gain,
    mix_shift,
    feed_gain,
    feed_shift,
    heads_bias,
    up_bias,
    heads_w,
    up_w,
    gathered,
    halo,
    frames,
    stacked,
    subsampled,
    mix_input,
    feed_input,
    heads_stage,
    up_stage,
    load_sem,
    halo_sem,
    send1,
    recv1,
    send2,
    recv2,
    send3,
    recv3,
    heads_sem,
    up_sem,
):
    group = lax.axis_index("groups")
    span = lax.axis_index("seq")
    lane = lax.axis_index("tensor")
    taps, width = conv_hbm.shape
    depth = gathered.shape[1]
    piece_rows = depth // 8
    rows = subsampled.shape[0]
    mels, mel_rows = spectrum.shape
    channels = subsampled.shape[1]

    core = lax.rem(span, 2)
    sibling = span + 1 - 2 * core
    across = lax.rem(span + 2, 4)
    other = 1 - group
    following = lax.rem(span + 1, 4)

    def load(index, source, target):
        return pltpu.make_async_copy(source, target, load_sem.at[index])

    load_conv = load(0, conv_hbm, gathered.at[lane, pl.ds(0, taps), :])
    load_conv_bias = load(1, conv_bias_hbm, conv_bias.at[0])
    load_spectrum = load(2, spectrum_hbm, spectrum)
    small = [
        (depth_weight_hbm, depth_weight),
        (depth_bias_hbm, depth_bias.at[0]),
        (mix_gain_hbm, mix_gain.at[0]),
        (mix_shift_hbm, mix_shift.at[0]),
        (feed_gain_hbm, feed_gain.at[0]),
        (feed_shift_hbm, feed_shift.at[0]),
        (heads_bias_hbm, heads_bias.at[0]),
        (up_bias_hbm, up_bias.at[0]),
    ]
    small = [load(3 + index, *pair) for index, pair in enumerate(small)]
    load_heads = load(11, heads_hbm, heads_w)
    load_up = load(12, up_hbm, up_w)
    load_conv.start()
    load_conv_bias.start()
    load_spectrum.start()

    barrier = pltpu.get_barrier_semaphore()
    peers = [(group, span, lax.rem(lane + k, count)) for k in range(1, count)]
    peers += [(group, sibling, lane), (group, across, lane), (group, 3 - span, lane)]
    peers += [(other, span, lane), (other, across, lane)]
    for peer in peers:
        pl.semaphore_signal(barrier, inc=1, device_id=peer, device_id_type=MESH)

    load_conv_bias.wait()
    bias = conv_bias[...]
    high = bias.astype(jnp.bfloat16).astype(jnp.float32)
    row_id = lax.broadcasted_iota(jnp.int32, (depth - taps, width), 0)
    bias_rows = jnp.where(row_id == 0, high, jnp.where(row_id == 1, bias - high, 0.0))
    gathered[lane, taps:depth, :] = bias_rows.astype(jnp.bfloat16)

    load_conv.wait()
    pl.semaphore_wait(barrier, len(peers))

    def piece(shard, owner_group, owner_span):
        start = pl.multiple_of((owner_group * 4 + owner_span) * piece_rows, piece_rows)
        return gathered.at[shard, pl.ds(start, piece_rows), :]

    def send(part, target, send_sem, recv_sem):
        return pltpu.make_async_remote_copy(
            src_ref=part,
            dst_ref=part,
            send_sem=send_sem,
            recv_sem=recv_sem,
            device_id=target,
            device_id_type=MESH,
        )

    sources = [lax.rem(lane + count - k, count) for k in range(1, count)]
    first = []
    for k in range(1, count):
        copy = send(
            piece(lane, group, span),
            (group, span, lax.rem(lane + k, count)),
            send1.at[k - 1],
            recv1.at[k - 1],
        )
        copy.start()
        first.append(copy)
    halo_copy = pltpu.make_async_remote_copy(
        src_ref=spectrum_hbm.at[:, pl.ds(mel_rows - HALO, HALO)],
        dst_ref=halo,
        send_sem=halo_sem.at[0],
        recv_sem=halo_sem.at[1],
        device_id=(group, following, lane),
        device_id_type=MESH,
    )
    halo_copy.start()
    for copy in small:
        copy.start()
    load_heads.start()
    load_up.start()

    load_spectrum.wait()
    frames[HALO : HALO + mel_rows, 0:mels] = spectrum[...].astype(jnp.float32).T

    chips = [(group, across), (other, span), (other, across)]
    second = []
    for k in range(count - 1):
        first[k].wait_recv()
        part = piece(sources[k], group, span)
        copies = []
        for j, (to_group, to_span) in enumerate(chips):
            copies.append(send(part, (to_group, to_span, lane), send2.at[k, j], recv2.at[k, j]))
        copies.append(send(part, (group, sibling, lane), send2.at[k, 3], recv2.at[k, 3]))
        for copy in copies:
            copy.start()
        second.append(copies)

    halo_copy.wait_recv()
    frames[0:HALO, 0:mels] = jnp.where(span == 0, 0.0, halo[...].astype(jnp.float32)).T

    def tap(offset):
        return frames[pl.ds(HALO + offset, rows, stride=4), :][:, 0:mels]

    taken = {offset: tap(offset) for offset in range(-3, 4)}
    tail_id = lax.broadcasted_iota(jnp.int32, (rows, depth - taps), 1)
    tail = jnp.where(tail_id < 2, 1.0, 0.0)
    row_zero = lax.broadcasted_iota(jnp.int32, (rows, depth - taps), 0) == 0
    start_tail = jnp.where(row_zero & (span == 0), 0.0, tail)
    for which, (base, end) in enumerate(((-3, start_tail), (-1, tail), (1, tail))):
        block = jnp.concatenate([taken[base], taken[base + 1], taken[base + 2], end], axis=1)
        stacked[which * rows : (which + 1) * rows, :] = block.astype(jnp.bfloat16)

    def conv_shard(shard):
        columns = pl.ds(pl.multiple_of(shard * width, 128), width)
        summed = jnp.dot(stacked[...], gathered[shard], preferred_element_type=jnp.float32)
        summed = jnp.maximum(summed, 0.0)
        total = (
            summed[0:rows] * depth_weight[0:1, columns]
            + summed[rows : 2 * rows] * depth_weight[1:2, columns]
            + summed[2 * rows :] * depth_weight[2:3, columns]
            + depth_bias[0:1, columns]
        )
        subsampled[:, columns] = jnp.maximum(total, 0.0).astype(jnp.bfloat16)

    for copy in small:
        copy.wait()
    conv_shard(lane)

    third = []
    for k in range(count - 1):
        copies = []
        for j, (to_group, to_span) in enumerate(chips):
            second[k][j].wait_recv()
            copy = send(
                piece(sources[k], to_group, to_span),
                (group, sibling, lane),
                send3.at[k, j],
                recv3.at[k, j],
            )
            copy.start()
            copies.append(copy)
        third.append(copies)

    for k in range(count - 1):
        second[k][3].wait_recv()
        for copy in third[k]:
            copy.wait_recv()
        conv_shard(sources[k])

    chunk = 32

    @pl.loop(0, rows // chunk)
    def _(step):
        some = pl.ds(pl.multiple_of(step * chunk, chunk), chunk)
        values = subsampled[some, :].astype(jnp.float32)
        centred = values - jnp.sum(values, axis=1, keepdims=True) * (1.0 / channels)
        variance = jnp.sum(centred * centred, axis=1, keepdims=True) * (1.0 / channels)
        normed = centred * lax.rsqrt(variance + epsilon)
        mix_input[some, :] = (normed * mix_gain[...] + mix_shift[...]).astype(jnp.bfloat16)
        feed_input[some, :] = (normed * feed_gain[...] + feed_shift[...]).astype(jnp.bfloat16)

    def project(source, weight, bias_row, stage, out, sem, loaded, activation):
        loaded.wait()
        tile = 256
        whole, rest = tiles_of(stage.shape[1], tile)

        def columns_copy(index, start, size):
            columns = pl.ds(start, size)
            return pltpu.make_async_copy(stage.at[:, columns], out.at[:, columns], sem.at[index])

        def one(index, start, size):
            columns = pl.ds(start, size)
            summed = jnp.dot(source[...], weight[:, columns], preferred_element_type=jnp.float32)
            summed = summed + bias_row[0:1, columns]
            stage[:, columns] = activation(summed).astype(jnp.bfloat16)
            columns_copy(index, start, size).start()

        @pl.loop(0, whole)
        def _(index):
            one(index, pl.multiple_of(index * tile, tile), tile)

        if rest:
            one(whole, whole * tile, rest)

        def finish():
            for index in range(whole):
                columns_copy(index, index * tile, tile).wait()
            if rest:
                columns_copy(whole, whole * tile, rest).wait()

        return finish

    finish_heads = project(
        mix_input, heads_w, heads_bias, heads_stage, heads_out, heads_sem, load_heads, lambda v: v
    )
    finish_up = project(
        feed_input, up_w, up_bias, up_stage, up_out, up_sem, load_up, jax.nn.silu
    )
    halo_copy.wait_send()
    for copy in first:
        copy.wait_send()
    for copies in second + third:
        for copy in copies:
            copy.wait_send()
    finish_heads()
    finish_up()


def kernel_device(
    count,
    spectrum,
    conv_weight,
    conv_bias,
    depth_weight,
    depth_bias,
    mix_gain,
    mix_shift,
    feed_gain,
    feed_shift,
    heads_weight,
    heads_bias,
    up_weight,
    up_bias,
):
    mel_rows, mels = spectrum.shape
    width = conv_weight.shape[2]
    channels = depth_weight.shape[1]
    taps = 3 * mels
    depth = -(-(taps + 2) // 256) * 256
    rows = mel_rows // 4
    heads_cols, up_cols = heads_weight.shape[1], up_weight.shape[1]
    hbm = pl.BlockSpec(memory_space=pltpu.HBM)
    anywhere = pl.BlockSpec(memory_space=pl.ANY)
    dma = pltpu.SemaphoreType.DMA
    bf16 = jnp.bfloat16
    return pl.pallas_call(
        functools.partial(front_kernel, count),
        out_shape=(
            jax.ShapeDtypeStruct((rows, heads_cols), bf16),
            jax.ShapeDtypeStruct((rows, up_cols), bf16),
        ),
        in_specs=[hbm] * 13,
        out_specs=(anywhere, anywhere),
        scratch_shapes=[
            pltpu.VMEM((mels, mel_rows), bf16),
            pltpu.VMEM((1, width), jnp.float32),
            pltpu.VMEM((3, channels), jnp.float32),
            pltpu.VMEM((1, channels), jnp.float32),
            pltpu.VMEM((1, channels), jnp.float32),
            pltpu.VMEM((1, channels), jnp.float32),
            pltpu.VMEM((1, channels), jnp.float32),
            pltpu.VMEM((1, channels), jnp.float32),
            pltpu.VMEM((1, heads_cols), jnp.float32),
            pltpu.VMEM((1, up_cols), jnp.float32),
            pltpu.VMEM((channels, heads_cols), bf16),
            pltpu.VMEM((channels, up_cols), bf16),
            pltpu.VMEM((count, depth, width), bf16),
            pltpu.VMEM((mels, HALO), bf16),
            pltpu.VMEM((HALO + mel_rows, 128), jnp.float32),
            pltpu.VMEM((3 * rows, depth), bf16),
            pltpu.VMEM((rows, channels), bf16),
            pltpu.VMEM((rows, channels), bf16),
            pltpu.VMEM((rows, channels), bf16),
            pltpu.VMEM((rows, heads_cols), bf16),
            pltpu.VMEM((rows, up_cols), bf16),
            dma((13,)),
            dma((2,)),
            dma((count - 1,)),
            dma((count - 1,)),
            dma((count - 1, 4)),
            dma((count - 1, 4)),
            dma((count - 1, 3)),
            dma((count - 1, 3)),
            dma((-(-heads_cols // 256),)),
            dma((-(-up_cols // 256),)),
        ],
        compiler_params=pltpu.CompilerParams(
            collective_id=0, has_side_effects=True, vmem_limit_bytes=64 * 2**20
        ),
        cost_estimate=pl.CostEstimate(
            flops=2 * rows * channels * (heads_cols + up_cols + 3 * taps),
            bytes_accessed=2 * (channels + rows) * (heads_cols + up_cols),
            transcendentals=rows * up_cols,
        ),
        name="front",
    )(
        spectrum.T,
        conv_weight.reshape(taps, width),
        conv_bias,
        depth_weight,
        depth_bias,
        mix_gain,
        mix_shift,
        feed_gain,
        feed_shift,
        heads_bias,
        up_bias,
        heads_weight,
        up_weight,
    )


def solution(mesh):
    in_specs = (
        P(("groups", "seq"), None),
        P(None, None, "tensor"),
        P("tensor"),
        P(),
        P(),
        P(),
        P(),
        P(),
        P(),
        P(None, "tensor"),
        P("tensor"),
        P(None, "tensor"),
        P("tensor"),
    )
    out_specs = (P(("groups", "seq"), "tensor"), P(("groups", "seq"), "tensor"))
    groups, spans, count = (mesh.shape[name] for name in ("groups", "seq", "tensor"))

    def per_device(*arrays):
        width = arrays[1].shape[2]
        if groups == 2 and spans == 4 and count > 1 and width % 128 == 0:
            return kernel_device(count, *arrays)
        return plain_device(*arrays)

    return jax.shard_map(
        per_device, mesh=mesh, in_specs=in_specs, out_specs=out_specs, check_vma=False
    )
```

```python
import functools

import jax
import jax.numpy as jnp
from jax import lax
from jax.experimental import pallas as pl
from jax.experimental.pallas import tpu as pltpu
from jax.sharding import PartitionSpec as P

epsilon = 1e-05
HALO = 128
MESH = pl.DeviceIdType.MESH


def passed_along(value, axis, steps):
    count = lax.axis_size(axis)
    initial, last = (max(0, -steps), min(count, count - steps))
    return lax.ppermute(value, axis, [(source, source + steps) for source in range(initial, last)])


def conv_rows(prior_rows, even_rows, odd_rows, conv_weight, conv_bias):
    stacked = jnp.concatenate([prior_rows, even_rows, odd_rows], axis=1)
    flat_weight = conv_weight.reshape(-1, conv_weight.shape[2])
    summed = jnp.dot(stacked, flat_weight, preferred_element_type=jnp.float32) + conv_bias
    return jax.nn.relu(summed).astype(jnp.bfloat16)


def first_conv(spectrum, prior_row, conv_weight, conv_bias):
    even_rows = spectrum[0::2]
    odd_rows = spectrum[1::2]
    prior_rows = jnp.concatenate([prior_row, odd_rows[:-1]], axis=0)
    return conv_rows(prior_rows, even_rows, odd_rows, conv_weight, conv_bias)


def depth_conv(channels, prior_row, depth_weight, depth_bias):
    even_half = channels[0::2].astype(jnp.float32)
    odd_half = channels[1::2].astype(jnp.float32)
    prior_half = jnp.concatenate([prior_row.astype(jnp.float32), odd_half[:-1]], axis=0)
    summed = (
        prior_half * depth_weight[0]
        + even_half * depth_weight[1]
        + odd_half * depth_weight[2]
        + depth_bias
    )
    return jax.nn.relu(summed).astype(jnp.bfloat16)


def plain_device(
    spectrum,
    conv_weight,
    conv_bias,
    depth_weight,
    depth_bias,
    mix_gain,
    mix_shift,
    feed_gain,
    feed_shift,
    heads_weight,
    heads_bias,
    up_weight,
    up_bias,
):
    mel_prior = passed_along(spectrum[-1:], "seq", 1)
    channels = first_conv(spectrum, mel_prior, conv_weight, conv_bias)
    own_width = channels.shape[1]
    lane_index = lax.axis_index("tensor")
    own_weight = lax.dynamic_slice_in_dim(depth_weight, lane_index * own_width, own_width, 1)
    own_bias = lax.dynamic_slice_in_dim(depth_bias, lane_index * own_width, own_width, 0)
    prior_row = passed_along(channels[-1:], "seq", 1)
    reduced = depth_conv(channels, prior_row, own_weight, own_bias)
    subsampled = lax.all_to_all(reduced, "tensor", split_axis=0, concat_axis=1, tiled=True)
    frames_float = lax.all_gather(subsampled, "tensor", axis=0, tiled=True).astype(jnp.float32)
    row_mean = jnp.mean(frames_float, axis=-1, keepdims=True)
    centred = frames_float - row_mean
    variance = jnp.mean(centred * centred, axis=-1, keepdims=True)
    normed = centred * lax.rsqrt(variance + epsilon)
    mix_input = (normed * mix_gain + mix_shift).astype(jnp.bfloat16)
    feed_input = (normed * feed_gain + feed_shift).astype(jnp.bfloat16)
    heads_out = (
        jnp.dot(mix_input, heads_weight, preferred_element_type=jnp.float32) + heads_bias
    ).astype(jnp.bfloat16)
    raised = jnp.dot(feed_input, up_weight, preferred_element_type=jnp.float32) + up_bias
    gated = jax.nn.silu(raised).astype(jnp.bfloat16)
    return heads_out, gated


def tiles_of(width, tile):
    whole = width // tile
    return whole, width - whole * tile


def front_kernel(
    count,
    spectrum_hbm,
    conv_hbm,
    conv_bias_hbm,
    depth_weight_hbm,
    depth_bias_hbm,
    subsampled_out,
    spectrum,
    conv_bias,
    depth_weight,
    depth_bias,
    gathered,
    halo,
    frames,
    stacked,
    subsampled,
    load_sem,
    halo_sem,
    send1,
    recv1,
    send2,
    recv2,
    send3,
    recv3,
    out_sem,
):
    group = lax.axis_index("groups")
    span = lax.axis_index("seq")
    lane = lax.axis_index("tensor")
    taps, width = conv_hbm.shape
    depth = gathered.shape[1]
    piece_rows = depth // 8
    rows = subsampled.shape[0]
    mels, mel_rows = spectrum.shape

    core = lax.rem(span, 2)
    sibling = span + 1 - 2 * core
    across = lax.rem(span + 2, 4)
    other = 1 - group
    following = lax.rem(span + 1, 4)

    def load(index, source, target):
        return pltpu.make_async_copy(source, target, load_sem.at[index])

    load_conv = load(0, conv_hbm, gathered.at[lane, pl.ds(0, taps), :])
    load_conv_bias = load(1, conv_bias_hbm, conv_bias.at[0])
    load_spectrum = load(2, spectrum_hbm, spectrum)
    small = [
        (depth_weight_hbm, depth_weight),
        (depth_bias_hbm, depth_bias.at[0]),
    ]
    small = [load(3 + index, *pair) for index, pair in enumerate(small)]
    load_conv.start()
    load_conv_bias.start()
    load_spectrum.start()

    barrier = pltpu.get_barrier_semaphore()
    peers = [(group, span, lax.rem(lane + k, count)) for k in range(1, count)]
    peers += [(group, sibling, lane), (group, across, lane), (group, 3 - span, lane)]
    peers += [(other, span, lane), (other, across, lane)]
    for peer in peers:
        pl.semaphore_signal(barrier, inc=1, device_id=peer, device_id_type=MESH)

    load_conv_bias.wait()
    bias = conv_bias[...]
    high = bias.astype(jnp.bfloat16).astype(jnp.float32)
    row_id = lax.broadcasted_iota(jnp.int32, (depth - taps, width), 0)
    bias_rows = jnp.where(row_id == 0, high, jnp.where(row_id == 1, bias - high, 0.0))
    gathered[lane, taps:depth, :] = bias_rows.astype(jnp.bfloat16)

    load_conv.wait()
    pl.semaphore_wait(barrier, len(peers))

    def piece(shard, owner_group, owner_span):
        start = pl.multiple_of((owner_group * 4 + owner_span) * piece_rows, piece_rows)
        return gathered.at[shard, pl.ds(start, piece_rows), :]

    def send(part, target, send_sem, recv_sem):
        return pltpu.make_async_remote_copy(
            src_ref=part,
            dst_ref=part,
            send_sem=send_sem,
            recv_sem=recv_sem,
            device_id=target,
            device_id_type=MESH,
        )

    sources = [lax.rem(lane + count - k, count) for k in range(1, count)]
    first = []
    for k in range(1, count):
        copy = send(
            piece(lane, group, span),
            (group, span, lax.rem(lane + k, count)),
            send1.at[k - 1],
            recv1.at[k - 1],
        )
        copy.start()
        first.append(copy)
    halo_copy = pltpu.make_async_remote_copy(
        src_ref=spectrum_hbm.at[:, pl.ds(mel_rows - HALO, HALO)],
        dst_ref=halo,
        send_sem=halo_sem.at[0],
        recv_sem=halo_sem.at[1],
        device_id=(group, following, lane),
        device_id_type=MESH,
    )
    halo_copy.start()
    for copy in small:
        copy.start()

    load_spectrum.wait()
    frames[HALO : HALO + mel_rows, 0:mels] = spectrum[...].astype(jnp.float32).T

    chips = [(group, across), (other, span), (other, across)]
    second = []
    for k in range(count - 1):
        first[k].wait_recv()
        part = piece(sources[k], group, span)
        copies = []
        for j, (to_group, to_span) in enumerate(chips):
            copies.append(send(part, (to_group, to_span, lane), send2.at[k, j], recv2.at[k, j]))
        copies.append(send(part, (group, sibling, lane), send2.at[k, 3], recv2.at[k, 3]))
        for copy in copies:
            copy.start()
        second.append(copies)

    halo_copy.wait_recv()
    frames[0:HALO, 0:mels] = jnp.where(span == 0, 0.0, halo[...].astype(jnp.float32)).T

    def tap(offset):
        return frames[pl.ds(HALO + offset, rows, stride=4), :][:, 0:mels]

    taken = {offset: tap(offset) for offset in range(-3, 4)}
    tail_id = lax.broadcasted_iota(jnp.int32, (rows, depth - taps), 1)
    tail = jnp.where(tail_id < 2, 1.0, 0.0)
    row_zero = lax.broadcasted_iota(jnp.int32, (rows, depth - taps), 0) == 0
    start_tail = jnp.where(row_zero & (span == 0), 0.0, tail)
    for which, (base, end) in enumerate(((-3, start_tail), (-1, tail), (1, tail))):
        block = jnp.concatenate([taken[base], taken[base + 1], taken[base + 2], end], axis=1)
        stacked[which * rows : (which + 1) * rows, :] = block.astype(jnp.bfloat16)

    def conv_shard(index, shard):
        columns = pl.ds(pl.multiple_of(shard * width, 128), width)
        summed = jnp.dot(stacked[...], gathered[shard], preferred_element_type=jnp.float32)
        summed = jnp.maximum(summed, 0.0)
        total = (
            summed[0:rows] * depth_weight[0:1, columns]
            + summed[rows : 2 * rows] * depth_weight[1:2, columns]
            + summed[2 * rows :] * depth_weight[2:3, columns]
            + depth_bias[0:1, columns]
        )
        subsampled[:, columns] = jnp.maximum(total, 0.0).astype(jnp.bfloat16)
        copy = pltpu.make_async_copy(
            subsampled.at[:, columns], subsampled_out.at[:, columns], out_sem.at[index]
        )
        copy.start()
        return copy

    for copy in small:
        copy.wait()
    stores = [conv_shard(0, lane)]

    third = []
    for k in range(count - 1):
        copies = []
        for j, (to_group, to_span) in enumerate(chips):
            second[k][j].wait_recv()
            copy = send(
                piece(sources[k], to_group, to_span),
                (group, sibling, lane),
                send3.at[k, j],
                recv3.at[k, j],
            )
            copy.start()
            copies.append(copy)
        third.append(copies)

    for k in range(count - 1):
        second[k][3].wait_recv()
        for copy in third[k]:
            copy.wait_recv()
        stores.append(conv_shard(k + 1, sources[k]))

    halo_copy.wait_send()
    for copy in first:
        copy.wait_send()
    for copies in second + third:
        for copy in copies:
            copy.wait_send()
    for copy in stores:
        copy.wait()


WEIGHT_PARTS = 4


def project_kernel(
    subsampled_hbm,
    mix_gain_hbm,
    mix_shift_hbm,
    feed_gain_hbm,
    feed_shift_hbm,
    heads_bias_hbm,
    up_bias_hbm,
    heads_hbm,
    up_hbm,
    heads_out,
    up_out,
    subsampled,
    mix_gain,
    mix_shift,
    feed_gain,
    feed_shift,
    heads_bias,
    up_bias,
    heads_w,
    up_w,
    mix_input,
    feed_input,
    heads_stage,
    up_stage,
    load_sem,
    heads_load,
    up_load,
    heads_sem,
    up_sem,
):
    rows, channels = subsampled.shape
    small = [
        (subsampled_hbm, subsampled),
        (mix_gain_hbm, mix_gain.at[0]),
        (mix_shift_hbm, mix_shift.at[0]),
        (feed_gain_hbm, feed_gain.at[0]),
        (feed_shift_hbm, feed_shift.at[0]),
        (heads_bias_hbm, heads_bias.at[0]),
        (up_bias_hbm, up_bias.at[0]),
    ]
    small = [
        pltpu.make_async_copy(source, target, load_sem.at[index])
        for index, (source, target) in enumerate(small)
    ]
    for copy in small:
        copy.start()

    def load_weight(source, target, sem):
        part = channels // WEIGHT_PARTS
        copies = []
        for index in range(WEIGHT_PARTS):
            some = pl.ds(index * part, part)
            copies.append(
                pltpu.make_async_copy(source.at[some, :], target.at[some, :], sem.at[index])
            )
            copies[-1].start()
        return copies

    heads_loads = load_weight(heads_hbm, heads_w, heads_load)
    up_loads = load_weight(up_hbm, up_w, up_load)
    for copy in small:
        copy.wait()

    chunk = 16

    @pl.loop(0, rows // chunk, unroll=4)
    def _(step):
        some = pl.ds(pl.multiple_of(step * chunk, chunk), chunk)
        values = subsampled[some, :].astype(jnp.float32)
        centred = values - jnp.sum(values, axis=1, keepdims=True) * (1.0 / channels)
        variance = jnp.sum(centred * centred, axis=1, keepdims=True) * (1.0 / channels)
        normed = centred * lax.rsqrt(variance + epsilon)
        mix_input[some, :] = (normed * mix_gain[...] + mix_shift[...]).astype(jnp.bfloat16)
        feed_input[some, :] = (normed * feed_gain[...] + feed_shift[...]).astype(jnp.bfloat16)

    def project(source, weight, bias_row, stage, out, sem, loaded, activation):
        for copy in loaded:
            copy.wait()
        tile = 256
        whole, rest = tiles_of(stage.shape[1], tile)

        def columns_copy(index, start, size):
            columns = pl.ds(start, size)
            return pltpu.make_async_copy(stage.at[:, columns], out.at[:, columns], sem.at[index])

        def one(index, start, size):
            columns = pl.ds(start, size)
            summed = jnp.dot(source[...], weight[:, columns], preferred_element_type=jnp.float32)
            summed = summed + bias_row[0:1, columns]
            stage[:, columns] = activation(summed).astype(jnp.bfloat16)
            columns_copy(index, start, size).start()

        for index in range(whole):
            one(index, index * tile, tile)

        if rest:
            one(whole, whole * tile, rest)

        def finish():
            for index in range(whole):
                columns_copy(index, index * tile, tile).wait()
            if rest:
                columns_copy(whole, whole * tile, rest).wait()

        return finish

    finish_heads = project(
        mix_input, heads_w, heads_bias, heads_stage, heads_out, heads_sem, heads_loads, lambda v: v
    )
    finish_up = project(
        feed_input, up_w, up_bias, up_stage, up_out, up_sem, up_loads, jax.nn.silu
    )
    finish_heads()
    finish_up()


def kernel_device(
    count,
    spectrum,
    conv_weight,
    conv_bias,
    depth_weight,
    depth_bias,
    mix_gain,
    mix_shift,
    feed_gain,
    feed_shift,
    heads_weight,
    heads_bias,
    up_weight,
    up_bias,
):
    mel_rows, mels = spectrum.shape
    width = conv_weight.shape[2]
    channels = depth_weight.shape[1]
    taps = 3 * mels
    depth = -(-(taps + 2) // 256) * 256
    rows = mel_rows // 4
    heads_cols, up_cols = heads_weight.shape[1], up_weight.shape[1]
    hbm = pl.BlockSpec(memory_space=pltpu.HBM)
    anywhere = pl.BlockSpec(memory_space=pl.ANY)
    dma = pltpu.SemaphoreType.DMA
    bf16 = jnp.bfloat16
    f32 = jnp.float32
    subsampled = pl.pallas_call(
        functools.partial(front_kernel, count),
        out_shape=jax.ShapeDtypeStruct((rows, channels), bf16),
        in_specs=[hbm] * 5,
        out_specs=anywhere,
        scratch_shapes=[
            pltpu.VMEM((mels, mel_rows), bf16),
            pltpu.VMEM((1, width), f32),
            pltpu.VMEM((3, channels), f32),
            pltpu.VMEM((1, channels), f32),
            pltpu.VMEM((count, depth, width), bf16),
            pltpu.VMEM((mels, HALO), bf16),
            pltpu.VMEM((HALO + mel_rows, 128), f32),
            pltpu.VMEM((3 * rows, depth), bf16),
            pltpu.VMEM((rows, channels), bf16),
            dma((5,)),
            dma((2,)),
            dma((count - 1,)),
            dma((count - 1,)),
            dma((count - 1, 4)),
            dma((count - 1, 4)),
            dma((count - 1, 3)),
            dma((count - 1, 3)),
            dma((count,)),
        ],
        compiler_params=pltpu.CompilerParams(
            collective_id=0, has_side_effects=True, vmem_limit_bytes=64 * 2**20
        ),
        cost_estimate=pl.CostEstimate(
            flops=2 * rows * channels * 3 * taps,
            bytes_accessed=2 * (mel_rows * mels + taps * width + rows * channels),
            transcendentals=0,
        ),
        name="front",
    )(
        spectrum.T,
        conv_weight.reshape(taps, width),
        conv_bias,
        depth_weight,
        depth_bias,
    )
    return pl.pallas_call(
        project_kernel,
        out_shape=(
            jax.ShapeDtypeStruct((rows, heads_cols), bf16),
            jax.ShapeDtypeStruct((rows, up_cols), bf16),
        ),
        in_specs=[hbm] * 9,
        out_specs=(hbm, hbm),
        scratch_shapes=[
            pltpu.VMEM((rows, channels), bf16),
            pltpu.VMEM((1, channels), f32),
            pltpu.VMEM((1, channels), f32),
            pltpu.VMEM((1, channels), f32),
            pltpu.VMEM((1, channels), f32),
            pltpu.VMEM((1, heads_cols), f32),
            pltpu.VMEM((1, up_cols), f32),
            pltpu.VMEM((channels, heads_cols), bf16),
            pltpu.VMEM((channels, up_cols), bf16),
            pltpu.VMEM((rows, channels), bf16),
            pltpu.VMEM((rows, channels), bf16),
            pltpu.VMEM((rows, heads_cols), bf16),
            pltpu.VMEM((rows, up_cols), bf16),
            dma((7,)),
            dma((WEIGHT_PARTS,)),
            dma((WEIGHT_PARTS,)),
            dma((-(-heads_cols // 256),)),
            dma((-(-up_cols // 256),)),
        ],
        compiler_params=pltpu.CompilerParams(vmem_limit_bytes=64 * 2**20),
        cost_estimate=pl.CostEstimate(
            flops=2 * rows * channels * (heads_cols + up_cols),
            bytes_accessed=2 * (channels + rows) * (heads_cols + up_cols),
            transcendentals=rows * up_cols,
        ),
        name="project",
    )(
        subsampled,
        mix_gain,
        mix_shift,
        feed_gain,
        feed_shift,
        heads_bias,
        up_bias,
        heads_weight,
        up_weight,
    )


def solution(mesh):
    in_specs = (
        P(("groups", "seq"), None),
        P(None, None, "tensor"),
        P("tensor"),
        P(),
        P(),
        P(),
        P(),
        P(),
        P(),
        P(None, "tensor"),
        P("tensor"),
        P(None, "tensor"),
        P("tensor"),
    )
    out_specs = (P(("groups", "seq"), "tensor"), P(("groups", "seq"), "tensor"))
    groups, spans, count = (mesh.shape[name] for name in ("groups", "seq", "tensor"))

    def per_device(*arrays):
        width = arrays[1].shape[2]
        if groups == 2 and spans == 4 and count > 1 and width % 128 == 0:
            return kernel_device(count, *arrays)
        return plain_device(*arrays)

    return jax.shard_map(
        per_device, mesh=mesh, in_specs=in_specs, out_specs=out_specs, check_vma=False
    )
```

```python
import functools

import jax
import jax.numpy as jnp
from jax import lax
from jax.experimental import pallas as pl
from jax.experimental.pallas import tpu as pltpu
from jax.sharding import PartitionSpec as P

epsilon = 1e-05
HALO = 128
MESH = pl.DeviceIdType.MESH


def passed_along(value, axis, steps):
    count = lax.axis_size(axis)
    initial, last = (max(0, -steps), min(count, count - steps))
    return lax.ppermute(value, axis, [(source, source + steps) for source in range(initial, last)])


def conv_rows(prior_rows, even_rows, odd_rows, conv_weight, conv_bias):
    stacked = jnp.concatenate([prior_rows, even_rows, odd_rows], axis=1)
    flat_weight = conv_weight.reshape(-1, conv_weight.shape[2])
    summed = jnp.dot(stacked, flat_weight, preferred_element_type=jnp.float32) + conv_bias
    return jax.nn.relu(summed).astype(jnp.bfloat16)


def first_conv(spectrum, prior_row, conv_weight, conv_bias):
    even_rows = spectrum[0::2]
    odd_rows = spectrum[1::2]
    prior_rows = jnp.concatenate([prior_row, odd_rows[:-1]], axis=0)
    return conv_rows(prior_rows, even_rows, odd_rows, conv_weight, conv_bias)


def depth_conv(channels, prior_row, depth_weight, depth_bias):
    even_half = channels[0::2].astype(jnp.float32)
    odd_half = channels[1::2].astype(jnp.float32)
    prior_half = jnp.concatenate([prior_row.astype(jnp.float32), odd_half[:-1]], axis=0)
    summed = (
        prior_half * depth_weight[0]
        + even_half * depth_weight[1]
        + odd_half * depth_weight[2]
        + depth_bias
    )
    return jax.nn.relu(summed).astype(jnp.bfloat16)


def plain_device(
    spectrum,
    conv_weight,
    conv_bias,
    depth_weight,
    depth_bias,
    mix_gain,
    mix_shift,
    feed_gain,
    feed_shift,
    heads_weight,
    heads_bias,
    up_weight,
    up_bias,
):
    mel_prior = passed_along(spectrum[-1:], "seq", 1)
    channels = first_conv(spectrum, mel_prior, conv_weight, conv_bias)
    own_width = channels.shape[1]
    lane_index = lax.axis_index("tensor")
    own_weight = lax.dynamic_slice_in_dim(depth_weight, lane_index * own_width, own_width, 1)
    own_bias = lax.dynamic_slice_in_dim(depth_bias, lane_index * own_width, own_width, 0)
    prior_row = passed_along(channels[-1:], "seq", 1)
    reduced = depth_conv(channels, prior_row, own_weight, own_bias)
    subsampled = lax.all_to_all(reduced, "tensor", split_axis=0, concat_axis=1, tiled=True)
    frames_float = lax.all_gather(subsampled, "tensor", axis=0, tiled=True).astype(jnp.float32)
    row_mean = jnp.mean(frames_float, axis=-1, keepdims=True)
    centred = frames_float - row_mean
    variance = jnp.mean(centred * centred, axis=-1, keepdims=True)
    normed = centred * lax.rsqrt(variance + epsilon)
    mix_input = (normed * mix_gain + mix_shift).astype(jnp.bfloat16)
    feed_input = (normed * feed_gain + feed_shift).astype(jnp.bfloat16)
    heads_out = (
        jnp.dot(mix_input, heads_weight, preferred_element_type=jnp.float32) + heads_bias
    ).astype(jnp.bfloat16)
    raised = jnp.dot(feed_input, up_weight, preferred_element_type=jnp.float32) + up_bias
    gated = jax.nn.silu(raised).astype(jnp.bfloat16)
    return heads_out, gated


def tiles_of(width, tile):
    whole = width // tile
    return whole, width - whole * tile


def front_kernel(
    count,
    spectrum_hbm,
    conv_hbm,
    conv_bias_hbm,
    depth_weight_hbm,
    depth_bias_hbm,
    subsampled_out,
    spectrum,
    conv_bias,
    depth_weight,
    depth_bias,
    gathered,
    halo,
    frames,
    stacked,
    subsampled,
    load_sem,
    halo_sem,
    send1,
    recv1,
    send2,
    recv2,
    send3,
    recv3,
    out_sem,
):
    group = lax.axis_index("groups")
    span = lax.axis_index("seq")
    lane = lax.axis_index("tensor")
    taps, width = conv_hbm.shape
    depth = gathered.shape[1]
    piece_rows = depth // 8
    rows = subsampled.shape[0]
    mels, mel_rows = spectrum.shape

    core = lax.rem(span, 2)
    sibling = span + 1 - 2 * core
    across = lax.rem(span + 2, 4)
    other = 1 - group
    following = lax.rem(span + 1, 4)

    def load(index, source, target):
        return pltpu.make_async_copy(source, target, load_sem.at[index])

    load_conv = load(0, conv_hbm, gathered.at[lane, pl.ds(0, taps), :])
    load_conv_bias = load(1, conv_bias_hbm, conv_bias.at[0])
    load_spectrum = load(2, spectrum_hbm, spectrum)
    small = [
        (depth_weight_hbm, depth_weight),
        (depth_bias_hbm, depth_bias.at[0]),
    ]
    small = [load(3 + index, *pair) for index, pair in enumerate(small)]
    load_conv.start()
    load_conv_bias.start()
    load_spectrum.start()

    barrier = pltpu.get_barrier_semaphore()
    peers = [(group, span, lax.rem(lane + k, count)) for k in range(1, count)]
    peers += [(group, sibling, lane), (group, across, lane), (group, 3 - span, lane)]
    peers += [(other, span, lane), (other, across, lane)]
    for peer in peers:
        pl.semaphore_signal(barrier, inc=1, device_id=peer, device_id_type=MESH)

    load_conv_bias.wait()
    bias = conv_bias[...]
    high = bias.astype(jnp.bfloat16).astype(jnp.float32)
    row_id = lax.broadcasted_iota(jnp.int32, (depth - taps, width), 0)
    bias_rows = jnp.where(row_id == 0, high, jnp.where(row_id == 1, bias - high, 0.0))
    gathered[lane, taps:depth, :] = bias_rows.astype(jnp.bfloat16)

    load_conv.wait()
    pl.semaphore_wait(barrier, len(peers))

    def piece(shard, owner_group, owner_span):
        start = pl.multiple_of((owner_group * 4 + owner_span) * piece_rows, piece_rows)
        return gathered.at[shard, pl.ds(start, piece_rows), :]

    def send(part, target, send_sem, recv_sem):
        return pltpu.make_async_remote_copy(
            src_ref=part,
            dst_ref=part,
            send_sem=send_sem,
            recv_sem=recv_sem,
            device_id=target,
            device_id_type=MESH,
        )

    sources = [lax.rem(lane + count - k, count) for k in range(1, count)]
    first = []
    for k in range(1, count):
        copy = send(
            piece(lane, group, span),
            (group, span, lax.rem(lane + k, count)),
            send1.at[k - 1],
            recv1.at[k - 1],
        )
        copy.start()
        first.append(copy)
    halo_copy = pltpu.make_async_remote_copy(
        src_ref=spectrum_hbm.at[:, pl.ds(mel_rows - HALO, HALO)],
        dst_ref=halo,
        send_sem=halo_sem.at[0],
        recv_sem=halo_sem.at[1],
        device_id=(group, following, lane),
        device_id_type=MESH,
    )
    halo_copy.start()
    for copy in small:
        copy.start()

    load_spectrum.wait()
    frames[HALO : HALO + mel_rows, 0:mels] = spectrum[...].astype(jnp.float32).T

    chips = [(group, across), (other, span), (other, across)]
    second = []
    for k in range(count - 1):
        first[k].wait_recv()
        part = piece(sources[k], group, span)
        copies = []
        for j, (to_group, to_span) in enumerate(chips):
            copies.append(send(part, (to_group, to_span, lane), send2.at[k, j], recv2.at[k, j]))
        copies.append(send(part, (group, sibling, lane), send2.at[k, 3], recv2.at[k, 3]))
        for copy in copies:
            copy.start()
        second.append(copies)

    halo_copy.wait_recv()
    frames[0:HALO, 0:mels] = jnp.where(span == 0, 0.0, halo[...].astype(jnp.float32)).T

    def tap(offset):
        return frames[pl.ds(HALO + offset, rows, stride=4), :][:, 0:mels]

    taken = {offset: tap(offset) for offset in range(-3, 4)}
    tail_id = lax.broadcasted_iota(jnp.int32, (rows, depth - taps), 1)
    tail = jnp.where(tail_id < 2, 1.0, 0.0)
    row_zero = lax.broadcasted_iota(jnp.int32, (rows, depth - taps), 0) == 0
    start_tail = jnp.where(row_zero & (span == 0), 0.0, tail)
    for which, (base, end) in enumerate(((-3, start_tail), (-1, tail), (1, tail))):
        block = jnp.concatenate([taken[base], taken[base + 1], taken[base + 2], end], axis=1)
        stacked[which * rows : (which + 1) * rows, :] = block.astype(jnp.bfloat16)

    def conv_shard(index, shard):
        columns = pl.ds(pl.multiple_of(shard * width, 128), width)
        summed = jnp.dot(stacked[...], gathered[shard], preferred_element_type=jnp.float32)
        summed = jnp.maximum(summed, 0.0)
        total = (
            summed[0:rows] * depth_weight[0:1, columns]
            + summed[rows : 2 * rows] * depth_weight[1:2, columns]
            + summed[2 * rows :] * depth_weight[2:3, columns]
            + depth_bias[0:1, columns]
        )
        subsampled[:, columns] = jnp.maximum(total, 0.0).astype(jnp.bfloat16)
        copy = pltpu.make_async_copy(
            subsampled.at[:, columns], subsampled_out.at[:, columns], out_sem.at[index]
        )
        copy.start()
        return copy

    for copy in small:
        copy.wait()
    stores = [conv_shard(0, lane)]

    third = []
    for k in range(count - 1):
        copies = []
        for j, (to_group, to_span) in enumerate(chips):
            second[k][j].wait_recv()
            copy = send(
                piece(sources[k], to_group, to_span),
                (group, sibling, lane),
                send3.at[k, j],
                recv3.at[k, j],
            )
            copy.start()
            copies.append(copy)
        third.append(copies)

    for k in range(count - 1):
        second[k][3].wait_recv()
        for copy in third[k]:
            copy.wait_recv()
        stores.append(conv_shard(k + 1, sources[k]))

    halo_copy.wait_send()
    for copy in first:
        copy.wait_send()
    for copies in second + third:
        for copy in copies:
            copy.wait_send()
    for copy in stores:
        copy.wait()


def project_kernel(
    subsampled,
    mix_gain_row,
    mix_shift_row,
    feed_gain_row,
    feed_shift_row,
    heads_bias_row,
    up_bias_row,
    heads_w,
    up_w,
    heads_out,
    up_out,
    mix_input,
    feed_input,
    heads_stage,
    up_stage,
    heads_sem,
    up_sem,
):
    rows, channels = subsampled.shape
    mix_gain, mix_shift, feed_gain, feed_shift, heads_bias, up_bias = (
        row[...].reshape(1, -1)
        for row in (
            mix_gain_row,
            mix_shift_row,
            feed_gain_row,
            feed_shift_row,
            heads_bias_row,
            up_bias_row,
        )
    )

    chunk = 16

    @pl.loop(0, rows // chunk, unroll=4)
    def _(step):
        some = pl.ds(pl.multiple_of(step * chunk, chunk), chunk)
        values = subsampled[some, :].astype(jnp.float32)
        centred = values - jnp.sum(values, axis=1, keepdims=True) * (1.0 / channels)
        variance = jnp.sum(centred * centred, axis=1, keepdims=True) * (1.0 / channels)
        normed = centred * lax.rsqrt(variance + epsilon)
        mix_input[some, :] = (normed * mix_gain + mix_shift).astype(jnp.bfloat16)
        feed_input[some, :] = (normed * feed_gain + feed_shift).astype(jnp.bfloat16)

    def project(source, weight, bias_row, stage, out, sem, activation):
        tile = 256
        whole, rest = tiles_of(stage.shape[1], tile)

        def columns_copy(index, start, size):
            columns = pl.ds(start, size)
            return pltpu.make_async_copy(stage.at[:, columns], out.at[:, columns], sem.at[index])

        def one(index, start, size):
            columns = pl.ds(start, size)
            summed = jnp.dot(source[...], weight[:, columns], preferred_element_type=jnp.float32)
            summed = summed + bias_row[:, start : start + size]
            stage[:, columns] = activation(summed).astype(jnp.bfloat16)
            columns_copy(index, start, size).start()

        for index in range(whole):
            one(index, index * tile, tile)

        if rest:
            one(whole, whole * tile, rest)

        def finish():
            for index in range(whole):
                columns_copy(index, index * tile, tile).wait()
            if rest:
                columns_copy(whole, whole * tile, rest).wait()

        return finish

    finish_heads = project(
        mix_input, heads_w, heads_bias, heads_stage, heads_out, heads_sem, lambda v: v
    )
    finish_up = project(
        feed_input, up_w, up_bias, up_stage, up_out, up_sem, jax.nn.silu
    )
    finish_heads()
    finish_up()


def kernel_device(
    count,
    spectrum,
    conv_weight,
    conv_bias,
    depth_weight,
    depth_bias,
    mix_gain,
    mix_shift,
    feed_gain,
    feed_shift,
    heads_weight,
    heads_bias,
    up_weight,
    up_bias,
):
    mel_rows, mels = spectrum.shape
    width = conv_weight.shape[2]
    channels = depth_weight.shape[1]
    taps = 3 * mels
    depth = -(-(taps + 2) // 256) * 256
    rows = mel_rows // 4
    heads_cols, up_cols = heads_weight.shape[1], up_weight.shape[1]
    hbm = pl.BlockSpec(memory_space=pltpu.HBM)
    vmem = pl.BlockSpec(memory_space=pltpu.VMEM)
    anywhere = pl.BlockSpec(memory_space=pl.ANY)
    dma = pltpu.SemaphoreType.DMA
    bf16 = jnp.bfloat16
    f32 = jnp.float32
    subsampled = pl.pallas_call(
        functools.partial(front_kernel, count),
        out_shape=jax.ShapeDtypeStruct((rows, channels), bf16),
        in_specs=[hbm] * 5,
        out_specs=anywhere,
        scratch_shapes=[
            pltpu.VMEM((mels, mel_rows), bf16),
            pltpu.VMEM((1, width), f32),
            pltpu.VMEM((3, channels), f32),
            pltpu.VMEM((1, channels), f32),
            pltpu.VMEM((count, depth, width), bf16),
            pltpu.VMEM((mels, HALO), bf16),
            pltpu.VMEM((HALO + mel_rows, 128), f32),
            pltpu.VMEM((3 * rows, depth), bf16),
            pltpu.VMEM((rows, channels), bf16),
            dma((5,)),
            dma((2,)),
            dma((count - 1,)),
            dma((count - 1,)),
            dma((count - 1, 4)),
            dma((count - 1, 4)),
            dma((count - 1, 3)),
            dma((count - 1, 3)),
            dma((count,)),
        ],
        compiler_params=pltpu.CompilerParams(
            collective_id=0, has_side_effects=True, vmem_limit_bytes=24 * 2**20
        ),
        cost_estimate=pl.CostEstimate(
            flops=16 * 2 * rows * channels * 3 * taps,
            bytes_accessed=32 * (mel_rows * mels + taps * width + rows * channels),
            transcendentals=0,
        ),
        name="front",
    )(
        *(
            pltpu.with_memory_space_constraint(array, pltpu.HBM)
            for array in (
                spectrum.T,
                conv_weight.reshape(taps, width),
                conv_bias,
                depth_weight,
                depth_bias,
            )
        )
    )
    return pl.pallas_call(
        project_kernel,
        out_shape=(
            jax.ShapeDtypeStruct((rows, heads_cols), bf16),
            jax.ShapeDtypeStruct((rows, up_cols), bf16),
        ),
        in_specs=[vmem] * 9,
        out_specs=(hbm, hbm),
        scratch_shapes=[
            pltpu.VMEM((rows, channels), bf16),
            pltpu.VMEM((rows, channels), bf16),
            pltpu.VMEM((rows, heads_cols), bf16),
            pltpu.VMEM((rows, up_cols), bf16),
            dma((-(-heads_cols // 256),)),
            dma((-(-up_cols // 256),)),
        ],
        compiler_params=pltpu.CompilerParams(vmem_limit_bytes=24 * 2**20),
        cost_estimate=pl.CostEstimate(
            flops=2 * rows * channels * (heads_cols + up_cols),
            bytes_accessed=2 * (channels + rows) * (heads_cols + up_cols),
            transcendentals=rows * up_cols,
        ),
        name="project",
    )(
        subsampled,
        pltpu.with_memory_space_constraint(mix_gain, pltpu.HBM),
        pltpu.with_memory_space_constraint(mix_shift, pltpu.HBM),
        pltpu.with_memory_space_constraint(feed_gain, pltpu.HBM),
        pltpu.with_memory_space_constraint(feed_shift, pltpu.HBM),
        pltpu.with_memory_space_constraint(heads_bias, pltpu.HBM),
        pltpu.with_memory_space_constraint(up_bias, pltpu.HBM),
        heads_weight,
        up_weight,
    )


def solution(mesh):
    in_specs = (
        P(("groups", "seq"), None),
        P(None, None, "tensor"),
        P("tensor"),
        P(),
        P(),
        P(),
        P(),
        P(),
        P(),
        P(None, "tensor"),
        P("tensor"),
        P(None, "tensor"),
        P("tensor"),
    )
    out_specs = (P(("groups", "seq"), "tensor"), P(("groups", "seq"), "tensor"))
    groups, spans, count = (mesh.shape[name] for name in ("groups", "seq", "tensor"))

    def per_device(*arrays):
        width = arrays[1].shape[2]
        if groups == 2 and spans == 4 and count > 1 and width % 128 == 0:
            return kernel_device(count, *arrays)
        return plain_device(*arrays)

    return jax.shard_map(
        per_device, mesh=mesh, in_specs=in_specs, out_specs=out_specs, check_vma=False
    )
```

```python
import functools

import jax
import jax.numpy as jnp
from jax import lax
from jax.experimental import pallas as pl
from jax.experimental.pallas import tpu as pltpu
from jax.sharding import PartitionSpec as P

epsilon = 1e-05
HALO = 128
MESH = pl.DeviceIdType.MESH


def passed_along(value, axis, steps):
    count = lax.axis_size(axis)
    initial, last = (max(0, -steps), min(count, count - steps))
    return lax.ppermute(value, axis, [(source, source + steps) for source in range(initial, last)])


def conv_rows(prior_rows, even_rows, odd_rows, conv_weight, conv_bias):
    stacked = jnp.concatenate([prior_rows, even_rows, odd_rows], axis=1)
    flat_weight = conv_weight.reshape(-1, conv_weight.shape[2])
    summed = jnp.dot(stacked, flat_weight, preferred_element_type=jnp.float32) + conv_bias
    return jax.nn.relu(summed).astype(jnp.bfloat16)


def first_conv(spectrum, prior_row, conv_weight, conv_bias):
    even_rows = spectrum[0::2]
    odd_rows = spectrum[1::2]
    prior_rows = jnp.concatenate([prior_row, odd_rows[:-1]], axis=0)
    return conv_rows(prior_rows, even_rows, odd_rows, conv_weight, conv_bias)


def depth_conv(channels, prior_row, depth_weight, depth_bias):
    even_half = channels[0::2].astype(jnp.float32)
    odd_half = channels[1::2].astype(jnp.float32)
    prior_half = jnp.concatenate([prior_row.astype(jnp.float32), odd_half[:-1]], axis=0)
    summed = (
        prior_half * depth_weight[0]
        + even_half * depth_weight[1]
        + odd_half * depth_weight[2]
        + depth_bias
    )
    return jax.nn.relu(summed).astype(jnp.bfloat16)


def plain_device(
    spectrum,
    conv_weight,
    conv_bias,
    depth_weight,
    depth_bias,
    mix_gain,
    mix_shift,
    feed_gain,
    feed_shift,
    heads_weight,
    heads_bias,
    up_weight,
    up_bias,
):
    mel_prior = passed_along(spectrum[-1:], "seq", 1)
    channels = first_conv(spectrum, mel_prior, conv_weight, conv_bias)
    own_width = channels.shape[1]
    lane_index = lax.axis_index("tensor")
    own_weight = lax.dynamic_slice_in_dim(depth_weight, lane_index * own_width, own_width, 1)
    own_bias = lax.dynamic_slice_in_dim(depth_bias, lane_index * own_width, own_width, 0)
    prior_row = passed_along(channels[-1:], "seq", 1)
    reduced = depth_conv(channels, prior_row, own_weight, own_bias)
    subsampled = lax.all_to_all(reduced, "tensor", split_axis=0, concat_axis=1, tiled=True)
    frames_float = lax.all_gather(subsampled, "tensor", axis=0, tiled=True).astype(jnp.float32)
    row_mean = jnp.mean(frames_float, axis=-1, keepdims=True)
    centred = frames_float - row_mean
    variance = jnp.mean(centred * centred, axis=-1, keepdims=True)
    normed = centred * lax.rsqrt(variance + epsilon)
    mix_input = (normed * mix_gain + mix_shift).astype(jnp.bfloat16)
    feed_input = (normed * feed_gain + feed_shift).astype(jnp.bfloat16)
    heads_out = (
        jnp.dot(mix_input, heads_weight, preferred_element_type=jnp.float32) + heads_bias
    ).astype(jnp.bfloat16)
    raised = jnp.dot(feed_input, up_weight, preferred_element_type=jnp.float32) + up_bias
    gated = jax.nn.silu(raised).astype(jnp.bfloat16)
    return heads_out, gated


def tiles_of(width, tile):
    whole = width // tile
    return whole, width - whole * tile


def front_kernel(
    count,
    spectrum_hbm,
    conv_hbm,
    conv_bias_hbm,
    depth_weight_hbm,
    depth_bias_hbm,
    subsampled_out,
    spectrum,
    conv_bias,
    depth_weight,
    depth_bias,
    gathered,
    halo,
    frames,
    stacked,
    subsampled,
    load_sem,
    halo_sem,
    send1,
    recv1,
    send2,
    recv2,
    send3,
    recv3,
    out_sem,
):
    group = lax.axis_index("groups")
    span = lax.axis_index("seq")
    lane = lax.axis_index("tensor")
    taps, width = conv_hbm.shape
    depth = gathered.shape[1]
    piece_rows = depth // 8
    rows = subsampled.shape[0]
    mels, mel_rows = spectrum.shape

    core = lax.rem(span, 2)
    sibling = span + 1 - 2 * core
    across = lax.rem(span + 2, 4)
    other = 1 - group
    following = lax.rem(span + 1, 4)

    def load(index, source, target):
        return pltpu.make_async_copy(source, target, load_sem.at[index])

    load_conv = load(0, conv_hbm, gathered.at[lane, pl.ds(0, taps), :])
    load_conv_bias = load(1, conv_bias_hbm, conv_bias.at[0])
    load_spectrum = load(2, spectrum_hbm, spectrum)
    small = [
        (depth_weight_hbm, depth_weight),
        (depth_bias_hbm, depth_bias.at[0]),
    ]
    small = [load(3 + index, *pair) for index, pair in enumerate(small)]
    load_conv.start()
    load_conv_bias.start()
    load_spectrum.start()
    for copy in small:
        copy.start()

    barrier = pltpu.get_barrier_semaphore()
    peers = [(group, span, lax.rem(lane + k, count)) for k in range(1, count)]
    peers += [(group, sibling, lane), (group, across, lane), (group, 3 - span, lane)]
    peers += [(other, span, lane), (other, across, lane)]
    for peer in peers:
        pl.semaphore_signal(barrier, inc=1, device_id=peer, device_id_type=MESH)

    load_conv_bias.wait()
    bias = conv_bias[...]
    high = bias.astype(jnp.bfloat16).astype(jnp.float32)
    row_id = lax.broadcasted_iota(jnp.int32, (depth - taps, width), 0)
    bias_rows = jnp.where(row_id == 0, high, jnp.where(row_id == 1, bias - high, 0.0))
    gathered[lane, taps:depth, :] = bias_rows.astype(jnp.bfloat16)

    def stack(some):
        taken = {
            offset: frames[pl.ds(HALO + offset, some, stride=4), :][:, 0:mels]
            for offset in range(-3, 4)
        }
        tail_id = lax.broadcasted_iota(jnp.int32, (some, depth - taps), 1)
        tail = jnp.where(tail_id < 2, 1.0, 0.0)
        row_zero = lax.broadcasted_iota(jnp.int32, (some, depth - taps), 0) == 0
        start_tail = jnp.where(row_zero & (span == 0), 0.0, tail)
        for which, (base, end) in enumerate(((-3, start_tail), (-1, tail), (1, tail))):
            block = jnp.concatenate([taken[base], taken[base + 1], taken[base + 2], end], axis=1)
            stacked[which * rows : which * rows + some, :] = block.astype(jnp.bfloat16)

    load_spectrum.wait()
    frames[0:HALO, :] = jnp.zeros((HALO, frames.shape[1]), jnp.float32)
    frames[HALO : HALO + mel_rows, 0:mels] = spectrum[...].astype(jnp.float32).T
    stack(rows)
    load_conv.wait()
    pl.semaphore_wait(barrier, len(peers))

    def piece(shard, owner_group, owner_span):
        start = pl.multiple_of((owner_group * 4 + owner_span) * piece_rows, piece_rows)
        return gathered.at[shard, pl.ds(start, piece_rows), :]

    def send(part, target, send_sem, recv_sem):
        return pltpu.make_async_remote_copy(
            src_ref=part,
            dst_ref=part,
            send_sem=send_sem,
            recv_sem=recv_sem,
            device_id=target,
            device_id_type=MESH,
        )

    sources = [lax.rem(lane + count - k, count) for k in range(1, count)]
    first = []
    for k in range(1, count):
        copy = send(
            piece(lane, group, span),
            (group, span, lax.rem(lane + k, count)),
            send1.at[k - 1],
            recv1.at[k - 1],
        )
        copy.start()
        first.append(copy)
    halo_copy = pltpu.make_async_remote_copy(
        src_ref=spectrum.at[:, pl.ds(mel_rows - HALO, HALO)],
        dst_ref=halo,
        send_sem=halo_sem.at[0],
        recv_sem=halo_sem.at[1],
        device_id=(group, following, lane),
        device_id_type=MESH,
    )
    halo_copy.start()


    chips = [(group, across), (other, span), (other, across)]
    second = []
    for k in range(count - 1):
        first[k].wait_recv()
        part = piece(sources[k], group, span)
        copies = []
        for j, (to_group, to_span) in enumerate(chips):
            copies.append(send(part, (to_group, to_span, lane), send2.at[k, j], recv2.at[k, j]))
        copies.append(send(part, (group, sibling, lane), send2.at[k, 3], recv2.at[k, 3]))
        for copy in copies:
            copy.start()
        second.append(copies)

    halo_copy.wait_recv()
    frames[0:HALO, 0:mels] = jnp.where(span == 0, 0.0, halo[...].astype(jnp.float32)).T
    stack(32)

    def conv_shard(index, shard):
        columns = pl.ds(pl.multiple_of(shard * width, 128), width)
        summed = jnp.dot(stacked[...], gathered[shard], preferred_element_type=jnp.float32)
        summed = jnp.maximum(summed, 0.0)
        total = (
            summed[0:rows] * depth_weight[0:1, columns]
            + summed[rows : 2 * rows] * depth_weight[1:2, columns]
            + summed[2 * rows :] * depth_weight[2:3, columns]
            + depth_bias[0:1, columns]
        )
        subsampled[:, columns] = jnp.maximum(total, 0.0).astype(jnp.bfloat16)
        copy = pltpu.make_async_copy(
            subsampled.at[:, columns], subsampled_out.at[:, columns], out_sem.at[index]
        )
        copy.start()
        return copy

    for copy in small:
        copy.wait()
    stores = [conv_shard(0, lane)]

    def finish_shard(k):
        second[k][3].wait_recv()
        for copy in third[k]:
            copy.wait_recv()
        stores.append(conv_shard(k + 1, sources[k]))

    third = []
    for k in range(count - 1):
        copies = []
        for j, (to_group, to_span) in enumerate(chips):
            second[k][j].wait_recv()
            copy = send(
                piece(sources[k], to_group, to_span),
                (group, sibling, lane),
                send3.at[k, j],
                recv3.at[k, j],
            )
            copy.start()
            copies.append(copy)
        third.append(copies)
        if k:
            finish_shard(k - 1)
    finish_shard(count - 2)
    halo_copy.wait_send()
    for copy in first:
        copy.wait_send()
    for copies in second + third:
        for copy in copies:
            copy.wait_send()
    for copy in stores:
        copy.wait()


def project_kernel(
    subsampled,
    mix_gain_row,
    mix_shift_row,
    feed_gain_row,
    feed_shift_row,
    heads_bias_row,
    up_bias_row,
    heads_w,
    up_w,
    heads_out,
    up_out,
    mix_input,
    feed_input,
    heads_stage,
    up_stage,
    heads_sem,
    up_sem,
):
    rows, channels = subsampled.shape
    mix_gain, mix_shift, feed_gain, feed_shift, heads_bias, up_bias = (
        row[...].reshape(1, -1)
        for row in (
            mix_gain_row,
            mix_shift_row,
            feed_gain_row,
            feed_shift_row,
            heads_bias_row,
            up_bias_row,
        )
    )

    chunk = 16

    @pl.loop(0, rows // chunk, unroll=4)
    def _(step):
        some = pl.ds(pl.multiple_of(step * chunk, chunk), chunk)
        values = subsampled[some, :].astype(jnp.float32)
        centred = values - jnp.sum(values, axis=1, keepdims=True) * (1.0 / channels)
        variance = jnp.sum(centred * centred, axis=1, keepdims=True) * (1.0 / channels)
        normed = centred * lax.rsqrt(variance + epsilon)
        mix_input[some, :] = (normed * mix_gain + mix_shift).astype(jnp.bfloat16)
        feed_input[some, :] = (normed * feed_gain + feed_shift).astype(jnp.bfloat16)

    def project(source, weight, bias_row, stage, out, sem, activation):
        tile = 256
        whole, rest = tiles_of(stage.shape[1], tile)

        def columns_copy(index, start, size):
            columns = pl.ds(start, size)
            return pltpu.make_async_copy(stage.at[:, columns], out.at[:, columns], sem.at[index])

        def one(index, start, size):
            columns = pl.ds(start, size)
            summed = jnp.dot(source[...], weight[:, columns], preferred_element_type=jnp.float32)
            summed = summed + bias_row[:, start : start + size]
            stage[:, columns] = activation(summed).astype(jnp.bfloat16)
            columns_copy(index, start, size).start()

        for index in range(whole):
            one(index, index * tile, tile)

        if rest:
            one(whole, whole * tile, rest)

        def finish():
            for index in range(whole):
                columns_copy(index, index * tile, tile).wait()
            if rest:
                columns_copy(whole, whole * tile, rest).wait()

        return finish

    finish_heads = project(
        mix_input, heads_w, heads_bias, heads_stage, heads_out, heads_sem, lambda v: v
    )
    finish_up = project(
        feed_input, up_w, up_bias, up_stage, up_out, up_sem, jax.nn.silu
    )
    finish_heads()
    finish_up()


def kernel_device(
    count,
    spectrum,
    conv_weight,
    conv_bias,
    depth_weight,
    depth_bias,
    mix_gain,
    mix_shift,
    feed_gain,
    feed_shift,
    heads_weight,
    heads_bias,
    up_weight,
    up_bias,
):
    mel_rows, mels = spectrum.shape
    width = conv_weight.shape[2]
    channels = depth_weight.shape[1]
    taps = 3 * mels
    depth = -(-(taps + 2) // 256) * 256
    rows = mel_rows // 4
    heads_cols, up_cols = heads_weight.shape[1], up_weight.shape[1]
    hbm = pl.BlockSpec(memory_space=pltpu.HBM)
    vmem = pl.BlockSpec(memory_space=pltpu.VMEM)
    anywhere = pl.BlockSpec(memory_space=pl.ANY)
    dma = pltpu.SemaphoreType.DMA
    bf16 = jnp.bfloat16
    f32 = jnp.float32
    subsampled = pl.pallas_call(
        functools.partial(front_kernel, count),
        out_shape=jax.ShapeDtypeStruct((rows, channels), bf16),
        in_specs=[hbm] * 5,
        out_specs=anywhere,
        scratch_shapes=[
            pltpu.VMEM((mels, mel_rows), bf16),
            pltpu.VMEM((1, width), f32),
            pltpu.VMEM((3, channels), f32),
            pltpu.VMEM((1, channels), f32),
            pltpu.VMEM((count, depth, width), bf16),
            pltpu.VMEM((mels, HALO), bf16),
            pltpu.VMEM((HALO + mel_rows, 128), f32),
            pltpu.VMEM((3 * rows, depth), bf16),
            pltpu.VMEM((rows, channels), bf16),
            dma((5,)),
            dma((2,)),
            dma((count - 1,)),
            dma((count - 1,)),
            dma((count - 1, 4)),
            dma((count - 1, 4)),
            dma((count - 1, 3)),
            dma((count - 1, 3)),
            dma((count,)),
        ],
        compiler_params=pltpu.CompilerParams(
            collective_id=0, has_side_effects=True, vmem_limit_bytes=24 * 2**20
        ),
        cost_estimate=pl.CostEstimate(
            flops=16 * 2 * rows * channels * 3 * taps,
            bytes_accessed=32 * (mel_rows * mels + taps * width + rows * channels),
            transcendentals=0,
        ),
        name="front",
    )(
        *(
            pltpu.with_memory_space_constraint(array, pltpu.HBM)
            for array in (
                spectrum.T,
                conv_weight.reshape(taps, width),
                conv_bias,
                depth_weight,
                depth_bias,
            )
        )
    )
    return pl.pallas_call(
        project_kernel,
        out_shape=(
            jax.ShapeDtypeStruct((rows, heads_cols), bf16),
            jax.ShapeDtypeStruct((rows, up_cols), bf16),
        ),
        in_specs=[vmem] * 9,
        out_specs=(hbm, hbm),
        scratch_shapes=[
            pltpu.VMEM((rows, channels), bf16),
            pltpu.VMEM((rows, channels), bf16),
            pltpu.VMEM((rows, heads_cols), bf16),
            pltpu.VMEM((rows, up_cols), bf16),
            dma((-(-heads_cols // 256),)),
            dma((-(-up_cols // 256),)),
        ],
        compiler_params=pltpu.CompilerParams(vmem_limit_bytes=24 * 2**20),
        cost_estimate=pl.CostEstimate(
            flops=2 * rows * channels * (heads_cols + up_cols),
            bytes_accessed=2 * (channels + rows) * (heads_cols + up_cols),
            transcendentals=rows * up_cols,
        ),
        name="project",
    )(
        subsampled,
        pltpu.with_memory_space_constraint(mix_gain, pltpu.HBM),
        pltpu.with_memory_space_constraint(mix_shift, pltpu.HBM),
        pltpu.with_memory_space_constraint(feed_gain, pltpu.HBM),
        pltpu.with_memory_space_constraint(feed_shift, pltpu.HBM),
        pltpu.with_memory_space_constraint(heads_bias, pltpu.HBM),
        pltpu.with_memory_space_constraint(up_bias, pltpu.HBM),
        heads_weight,
        up_weight,
    )


def solution(mesh):
    in_specs = (
        P(("groups", "seq"), None),
        P(None, None, "tensor"),
        P("tensor"),
        P(),
        P(),
        P(),
        P(),
        P(),
        P(),
        P(None, "tensor"),
        P("tensor"),
        P(None, "tensor"),
        P("tensor"),
    )
    out_specs = (P(("groups", "seq"), "tensor"), P(("groups", "seq"), "tensor"))
    groups, spans, count = (mesh.shape[name] for name in ("groups", "seq", "tensor"))

    def per_device(*arrays):
        width = arrays[1].shape[2]
        if groups == 2 and spans == 4 and count > 1 and width % 128 == 0:
            return kernel_device(count, *arrays)
        return plain_device(*arrays)

    return jax.shard_map(
        per_device, mesh=mesh, in_specs=in_specs, out_specs=out_specs, check_vma=False
    )
```

```python
import functools

import jax
import jax.numpy as jnp
from jax import lax
from jax.experimental import pallas as pl
from jax.experimental.pallas import tpu as pltpu
from jax.sharding import PartitionSpec as P

epsilon = 1e-05
HALO = 128
MESH = pl.DeviceIdType.MESH


def passed_along(value, axis, steps):
    count = lax.axis_size(axis)
    initial, last = (max(0, -steps), min(count, count - steps))
    return lax.ppermute(value, axis, [(source, source + steps) for source in range(initial, last)])


def conv_rows(prior_rows, even_rows, odd_rows, conv_weight, conv_bias):
    stacked = jnp.concatenate([prior_rows, even_rows, odd_rows], axis=1)
    flat_weight = conv_weight.reshape(-1, conv_weight.shape[2])
    summed = jnp.dot(stacked, flat_weight, preferred_element_type=jnp.float32) + conv_bias
    return jax.nn.relu(summed).astype(jnp.bfloat16)


def first_conv(spectrum, prior_row, conv_weight, conv_bias):
    even_rows = spectrum[0::2]
    odd_rows = spectrum[1::2]
    prior_rows = jnp.concatenate([prior_row, odd_rows[:-1]], axis=0)
    return conv_rows(prior_rows, even_rows, odd_rows, conv_weight, conv_bias)


def depth_conv(channels, prior_row, depth_weight, depth_bias):
    even_half = channels[0::2].astype(jnp.float32)
    odd_half = channels[1::2].astype(jnp.float32)
    prior_half = jnp.concatenate([prior_row.astype(jnp.float32), odd_half[:-1]], axis=0)
    summed = (
        prior_half * depth_weight[0]
        + even_half * depth_weight[1]
        + odd_half * depth_weight[2]
        + depth_bias
    )
    return jax.nn.relu(summed).astype(jnp.bfloat16)


def plain_device(
    spectrum,
    conv_weight,
    conv_bias,
    depth_weight,
    depth_bias,
    mix_gain,
    mix_shift,
    feed_gain,
    feed_shift,
    heads_weight,
    heads_bias,
    up_weight,
    up_bias,
):
    mel_prior = passed_along(spectrum[-1:], "seq", 1)
    channels = first_conv(spectrum, mel_prior, conv_weight, conv_bias)
    own_width = channels.shape[1]
    lane_index = lax.axis_index("tensor")
    own_weight = lax.dynamic_slice_in_dim(depth_weight, lane_index * own_width, own_width, 1)
    own_bias = lax.dynamic_slice_in_dim(depth_bias, lane_index * own_width, own_width, 0)
    prior_row = passed_along(channels[-1:], "seq", 1)
    reduced = depth_conv(channels, prior_row, own_weight, own_bias)
    subsampled = lax.all_to_all(reduced, "tensor", split_axis=0, concat_axis=1, tiled=True)
    frames_float = lax.all_gather(subsampled, "tensor", axis=0, tiled=True).astype(jnp.float32)
    row_mean = jnp.mean(frames_float, axis=-1, keepdims=True)
    centred = frames_float - row_mean
    variance = jnp.mean(centred * centred, axis=-1, keepdims=True)
    normed = centred * lax.rsqrt(variance + epsilon)
    mix_input = (normed * mix_gain + mix_shift).astype(jnp.bfloat16)
    feed_input = (normed * feed_gain + feed_shift).astype(jnp.bfloat16)
    heads_out = (
        jnp.dot(mix_input, heads_weight, preferred_element_type=jnp.float32) + heads_bias
    ).astype(jnp.bfloat16)
    raised = jnp.dot(feed_input, up_weight, preferred_element_type=jnp.float32) + up_bias
    gated = jax.nn.silu(raised).astype(jnp.bfloat16)
    return heads_out, gated


def tiles_of(width, tile):
    whole = width // tile
    return whole, width - whole * tile


def front_kernel(
    count,
    spectrum_hbm,
    conv_hbm,
    conv_bias_hbm,
    depth_weight_hbm,
    depth_bias_hbm,
    subsampled_out,
    spectrum,
    conv_bias,
    depth_weight,
    depth_bias,
    gathered,
    halo,
    frames,
    stacked,
    subsampled,
    load_sem,
    halo_sem,
    send1,
    recv1,
    send2,
    recv2,
    send3,
    recv3,
    out_sem,
):
    group = lax.axis_index("groups")
    span = lax.axis_index("seq")
    lane = lax.axis_index("tensor")
    taps, width = conv_hbm.shape
    depth = gathered.shape[1]
    piece_rows = depth // 8
    rows = subsampled.shape[0]
    mels, mel_rows = spectrum.shape

    core = lax.rem(span, 2)
    sibling = span + 1 - 2 * core
    across = lax.rem(span + 2, 4)
    other = 1 - group
    following = lax.rem(span + 1, 4)

    def load(index, source, target):
        return pltpu.make_async_copy(source, target, load_sem.at[index])

    load_conv = load(0, conv_hbm, gathered.at[lane, pl.ds(0, taps), :])
    load_conv_bias = load(1, conv_bias_hbm, conv_bias.at[0])
    load_spectrum = load(2, spectrum_hbm, spectrum)
    small = [
        (depth_weight_hbm, depth_weight),
        (depth_bias_hbm, depth_bias.at[0]),
    ]
    small = [load(3 + index, *pair) for index, pair in enumerate(small)]
    load_conv.start()
    load_conv_bias.start()
    load_spectrum.start()

    barrier = pltpu.get_barrier_semaphore()
    peers = [(group, span, lax.rem(lane + k, count)) for k in range(1, count)]
    peers += [(group, sibling, lane), (group, across, lane), (group, 3 - span, lane)]
    peers += [(other, span, lane), (other, across, lane)]
    for peer in peers:
        pl.semaphore_signal(barrier, inc=1, device_id=peer, device_id_type=MESH)

    load_conv_bias.wait()
    bias = conv_bias[...]
    high = bias.astype(jnp.bfloat16).astype(jnp.float32)
    row_id = lax.broadcasted_iota(jnp.int32, (depth - taps, width), 0)
    bias_rows = jnp.where(row_id == 0, high, jnp.where(row_id == 1, bias - high, 0.0))
    gathered[lane, taps:depth, :] = bias_rows.astype(jnp.bfloat16)

    load_conv.wait()
    pl.semaphore_wait(barrier, len(peers))

    def piece(shard, owner_group, owner_span):
        start = pl.multiple_of((owner_group * 4 + owner_span) * piece_rows, piece_rows)
        return gathered.at[shard, pl.ds(start, piece_rows), :]

    def send(part, target, send_sem, recv_sem):
        return pltpu.make_async_remote_copy(
            src_ref=part,
            dst_ref=part,
            send_sem=send_sem,
            recv_sem=recv_sem,
            device_id=target,
            device_id_type=MESH,
        )

    sources = [lax.rem(lane + count - k, count) for k in range(1, count)]
    first = []
    for k in range(1, count):
        copy = send(
            piece(lane, group, span),
            (group, span, lax.rem(lane + k, count)),
            send1.at[k - 1],
            recv1.at[k - 1],
        )
        copy.start()
        first.append(copy)
    halo_copy = pltpu.make_async_remote_copy(
        src_ref=spectrum_hbm.at[:, pl.ds(mel_rows - HALO, HALO)],
        dst_ref=halo,
        send_sem=halo_sem.at[0],
        recv_sem=halo_sem.at[1],
        device_id=(group, following, lane),
        device_id_type=MESH,
    )
    halo_copy.start()
    for copy in small:
        copy.start()


    chips = [(group, across), (other, span), (other, across)]
    second = []
    for k in range(count - 1):
        first[k].wait_recv()
        part = piece(sources[k], group, span)
        copies = []
        for j, (to_group, to_span) in enumerate(chips):
            copies.append(send(part, (to_group, to_span, lane), send2.at[k, j], recv2.at[k, j]))
        copies.append(send(part, (group, sibling, lane), send2.at[k, 3], recv2.at[k, 3]))
        for copy in copies:
            copy.start()
        second.append(copies)

    load_spectrum.wait()
    frames[HALO : HALO + mel_rows, 0:mels] = spectrum[...].astype(jnp.float32).T
    halo_copy.wait_recv()
    frames[0:HALO, 0:mels] = jnp.where(span == 0, 0.0, halo[...].astype(jnp.float32)).T

    def tap(offset):
        return frames[pl.ds(HALO + offset, rows, stride=4), :][:, 0:mels]

    taken = {offset: tap(offset) for offset in range(-3, 4)}
    tail_id = lax.broadcasted_iota(jnp.int32, (rows, depth - taps), 1)
    tail = jnp.where(tail_id < 2, 1.0, 0.0)
    row_zero = lax.broadcasted_iota(jnp.int32, (rows, depth - taps), 0) == 0
    start_tail = jnp.where(row_zero & (span == 0), 0.0, tail)
    for which, (base, end) in enumerate(((-3, start_tail), (-1, tail), (1, tail))):
        block = jnp.concatenate([taken[base], taken[base + 1], taken[base + 2], end], axis=1)
        stacked[which * rows : (which + 1) * rows, :] = block.astype(jnp.bfloat16)

    def conv_shard(index, shard):
        columns = pl.ds(pl.multiple_of(shard * width, 128), width)
        summed = jnp.dot(stacked[...], gathered[shard], preferred_element_type=jnp.float32)
        summed = jnp.maximum(summed, 0.0)
        total = (
            summed[0:rows] * depth_weight[0:1, columns]
            + summed[rows : 2 * rows] * depth_weight[1:2, columns]
            + summed[2 * rows :] * depth_weight[2:3, columns]
            + depth_bias[0:1, columns]
        )
        subsampled[:, columns] = jnp.maximum(total, 0.0).astype(jnp.bfloat16)
        copy = pltpu.make_async_copy(
            subsampled.at[:, columns], subsampled_out.at[:, columns], out_sem.at[index]
        )
        copy.start()
        return copy

    for copy in small:
        copy.wait()
    stores = [conv_shard(0, lane)]

    def finish_shard(k):
        second[k][3].wait_recv()
        for copy in third[k]:
            copy.wait_recv()
        stores.append(conv_shard(k + 1, sources[k]))

    third = []
    for k in range(count - 1):
        copies = []
        for j, (to_group, to_span) in enumerate(chips):
            second[k][j].wait_recv()
            copy = send(
                piece(sources[k], to_group, to_span),
                (group, sibling, lane),
                send3.at[k, j],
                recv3.at[k, j],
            )
            copy.start()
            copies.append(copy)
        third.append(copies)
        if k:
            finish_shard(k - 1)
    finish_shard(count - 2)
    halo_copy.wait_send()
    for copy in first:
        copy.wait_send()
    for copies in second + third:
        for copy in copies:
            copy.wait_send()
    for copy in stores:
        copy.wait()


def project_kernel(
    subsampled,
    mix_gain_row,
    mix_shift_row,
    feed_gain_row,
    feed_shift_row,
    heads_bias_row,
    up_bias_row,
    heads_w,
    up_w,
    heads_out,
    up_out,
    mix_input,
    feed_input,
    heads_stage,
    up_stage,
    heads_sem,
    up_sem,
):
    rows, channels = subsampled.shape
    mix_gain, mix_shift, feed_gain, feed_shift, heads_bias, up_bias = (
        row[...].reshape(1, -1)
        for row in (
            mix_gain_row,
            mix_shift_row,
            feed_gain_row,
            feed_shift_row,
            heads_bias_row,
            up_bias_row,
        )
    )

    chunk = 16

    @pl.loop(0, rows // chunk, unroll=4)
    def _(step):
        some = pl.ds(pl.multiple_of(step * chunk, chunk), chunk)
        values = subsampled[some, :].astype(jnp.float32)
        centred = values - jnp.sum(values, axis=1, keepdims=True) * (1.0 / channels)
        variance = jnp.sum(centred * centred, axis=1, keepdims=True) * (1.0 / channels)
        normed = centred * lax.rsqrt(variance + epsilon)
        mix_input[some, :] = (normed * mix_gain + mix_shift).astype(jnp.bfloat16)
        feed_input[some, :] = (normed * feed_gain + feed_shift).astype(jnp.bfloat16)

    def project(source, weight, bias_row, stage, out, sem, activation):
        tile = 256
        whole, rest = tiles_of(stage.shape[1], tile)

        def columns_copy(index, start, size):
            columns = pl.ds(start, size)
            return pltpu.make_async_copy(stage.at[:, columns], out.at[:, columns], sem.at[index])

        def one(index, start, size):
            columns = pl.ds(start, size)
            summed = jnp.dot(source[...], weight[:, columns], preferred_element_type=jnp.float32)
            summed = summed + bias_row[:, start : start + size]
            stage[:, columns] = activation(summed).astype(jnp.bfloat16)
            columns_copy(index, start, size).start()

        for index in range(whole):
            one(index, index * tile, tile)

        if rest:
            one(whole, whole * tile, rest)

        def finish():
            for index in range(whole):
                columns_copy(index, index * tile, tile).wait()
            if rest:
                columns_copy(whole, whole * tile, rest).wait()

        return finish

    finish_heads = project(
        mix_input, heads_w, heads_bias, heads_stage, heads_out, heads_sem, lambda v: v
    )
    finish_up = project(
        feed_input, up_w, up_bias, up_stage, up_out, up_sem, jax.nn.silu
    )
    finish_heads()
    finish_up()


def kernel_device(
    count,
    spectrum,
    conv_weight,
    conv_bias,
    depth_weight,
    depth_bias,
    mix_gain,
    mix_shift,
    feed_gain,
    feed_shift,
    heads_weight,
    heads_bias,
    up_weight,
    up_bias,
):
    mel_rows, mels = spectrum.shape
    width = conv_weight.shape[2]
    channels = depth_weight.shape[1]
    taps = 3 * mels
    depth = -(-(taps + 2) // 256) * 256
    rows = mel_rows // 4
    heads_cols, up_cols = heads_weight.shape[1], up_weight.shape[1]
    hbm = pl.BlockSpec(memory_space=pltpu.HBM)
    vmem = pl.BlockSpec(memory_space=pltpu.VMEM)
    anywhere = pl.BlockSpec(memory_space=pl.ANY)
    dma = pltpu.SemaphoreType.DMA
    bf16 = jnp.bfloat16
    f32 = jnp.float32
    subsampled = pl.pallas_call(
        functools.partial(front_kernel, count),
        out_shape=jax.ShapeDtypeStruct((rows, channels), bf16),
        in_specs=[hbm] * 5,
        out_specs=anywhere,
        scratch_shapes=[
            pltpu.VMEM((mels, mel_rows), bf16),
            pltpu.VMEM((1, width), f32),
            pltpu.VMEM((3, channels), f32),
            pltpu.VMEM((1, channels), f32),
            pltpu.VMEM((count, depth, width), bf16),
            pltpu.VMEM((mels, HALO), bf16),
            pltpu.VMEM((HALO + mel_rows, 128), f32),
            pltpu.VMEM((3 * rows, depth), bf16),
            pltpu.VMEM((rows, channels), bf16),
            dma((5,)),
            dma((2,)),
            dma((count - 1,)),
            dma((count - 1,)),
            dma((count - 1, 4)),
            dma((count - 1, 4)),
            dma((count - 1, 3)),
            dma((count - 1, 3)),
            dma((count,)),
        ],
        compiler_params=pltpu.CompilerParams(
            collective_id=0, has_side_effects=True, vmem_limit_bytes=24 * 2**20
        ),
        cost_estimate=pl.CostEstimate(
            flops=16 * 2 * rows * channels * 3 * taps,
            bytes_accessed=32 * (mel_rows * mels + taps * width + rows * channels),
            transcendentals=0,
        ),
        name="front",
    )(
        *(
            pltpu.with_memory_space_constraint(array, pltpu.HBM)
            for array in (
                spectrum.T,
                conv_weight.reshape(taps, width),
                conv_bias,
                depth_weight,
                depth_bias,
            )
        )
    )
    return pl.pallas_call(
        project_kernel,
        out_shape=(
            jax.ShapeDtypeStruct((rows, heads_cols), bf16),
            jax.ShapeDtypeStruct((rows, up_cols), bf16),
        ),
        in_specs=[vmem] * 9,
        out_specs=(hbm, hbm),
        scratch_shapes=[
            pltpu.VMEM((rows, channels), bf16),
            pltpu.VMEM((rows, channels), bf16),
            pltpu.VMEM((rows, heads_cols), bf16),
            pltpu.VMEM((rows, up_cols), bf16),
            dma((-(-heads_cols // 256),)),
            dma((-(-up_cols // 256),)),
        ],
        compiler_params=pltpu.CompilerParams(vmem_limit_bytes=24 * 2**20),
        cost_estimate=pl.CostEstimate(
            flops=2 * rows * channels * (heads_cols + up_cols),
            bytes_accessed=2 * (channels + rows) * (heads_cols + up_cols),
            transcendentals=rows * up_cols,
        ),
        name="project",
    )(
        subsampled,
        pltpu.with_memory_space_constraint(mix_gain, pltpu.HBM),
        pltpu.with_memory_space_constraint(mix_shift, pltpu.HBM),
        pltpu.with_memory_space_constraint(feed_gain, pltpu.HBM),
        pltpu.with_memory_space_constraint(feed_shift, pltpu.HBM),
        pltpu.with_memory_space_constraint(heads_bias, pltpu.HBM),
        pltpu.with_memory_space_constraint(up_bias, pltpu.HBM),
        heads_weight,
        up_weight,
    )


def solution(mesh):
    in_specs = (
        P(("groups", "seq"), None),
        P(None, None, "tensor"),
        P("tensor"),
        P(),
        P(),
        P(),
        P(),
        P(),
        P(),
        P(None, "tensor"),
        P("tensor"),
        P(None, "tensor"),
        P("tensor"),
    )
    out_specs = (P(("groups", "seq"), "tensor"), P(("groups", "seq"), "tensor"))
    groups, spans, count = (mesh.shape[name] for name in ("groups", "seq", "tensor"))

    def per_device(*arrays):
        width = arrays[1].shape[2]
        if groups == 2 and spans == 4 and count > 1 and width % 128 == 0:
            return kernel_device(count, *arrays)
        return plain_device(*arrays)

    return jax.shard_map(
        per_device, mesh=mesh, in_specs=in_specs, out_specs=out_specs, check_vma=False
    )
```
